256 devices in a mesh: dp: 32 (over x, y, core), tensor: 8 (over z).
Axes of the slice: x: 4, y: 4, z: 8, core: 2. Of those that a mesh axis runs over, the one named last changes fastest.
Arguments:
- patches: bfloat16 [32768, 1280], P('dp'), may hold values from -6 to 6
- vit_gain: float32 [1280], replicated, may hold values from 0.5 to 1.5
- fc_in: bfloat16 [1280, 5120], P(None, 'tensor'), may hold values from -0.15625 to 0.15625
- fc_out: bfloat16 [5120, 1280], P('tensor'), may hold values from -0.078125 to 0.078125
- merge_gain: float32 [1280], replicated, may hold values from 0.5 to 1.5
- merge_shift: float32 [1280], replicated, may hold values from -3 to 3
- merger: bfloat16 [5120, 8192], P('dp', 'tensor'), may hold values from -0.078125 to 0.078125
- counts: int32 [32, 32], replicated, may hold values from 0 to 16, as said below
- grad_packed: bfloat16 [16384, 8192], P('dp', 'tensor'), may hold values from -6 to 6
Outputs:
- visual: bfloat16 [16384, 8192], P('dp', 'tensor')
- grad_weight: float32 [5120, 8192], P('dp', 'tensor')
- grad_layer: float32 [32768, 1280], P(('dp', 'tensor'))
The draws below stay inside these ranges and needn't reach their ends.
Inputs may be any that keep to these rules, and one draw needn't show every extreme that they name: counts[s, d] is the number of merged tokens that dp index s sends to dp index d, taken in order from s's 256 tokens; every row sums to 256 and holds the value 16 at least once.
All inputs are finite; a program needn't handle non-finite values.
Results may differ from the reference program's by a relative error of at most 0.023.
Values may be sent and summed in bfloat16 or wider, within the bound.
No kernel may reach another device: no remote copies, remote signals or barrier semaphores. Data moves between devices by JAX's collectives and lax.ppermute only.
A program may use at most 128 MiB of HBM per device.

```python
import math
import jax
import jax.numpy as jnp
from jax import lax

D_V = 1280
FF_V = 5120
D_L = 8192
TOK_DEV = 256
MERGED = 5120
PATCHES = 32768
TOKENS = 8192
CAP = 16
RECV = 512
N_DP = 32
N_TENSOR = 8


def draw_counts(key, part):
    key = jax.random.fold_in(key, 7)
    half_count = N_DP // 2
    lower_part = jax.random.randint(key, (N_DP, half_count), 0, CAP + 1)
    lower_part = lower_part.at[:, 0].set(0)
    paired = jnp.concatenate([lower_part, CAP - lower_part], axis=1).astype(jnp.int32)
    key_list = jax.random.split(jax.random.fold_in(key, 1), N_DP)

    def shuffle_row(row_key, row_values):
        return jax.random.permutation(row_key, row_values)
    return jax.vmap(shuffle_row)(key_list, paired).astype(jnp.int32)


def levels(stream_key, extent, cuts, smallest, largest):
    loudness = 1.0
    for dim, parts in cuts:
        steps = jax.random.uniform(jax.random.fold_in(jax.random.fold_in(stream_key, 6), dim), (parts,), jnp.float32, smallest / len(cuts), largest / len(cuts))
        loudness = loudness * jnp.repeat(jnp.exp(steps), extent[dim] // parts).reshape((-1,) + (1,) * (len(extent) - 1 - dim))
    return loudness


def noise(stream_key, dims, deviation, reach, cuts=(), kind=jnp.bfloat16):
    result = deviation * jax.random.normal(stream_key, dims, jnp.float32)
    if cuts:
        result = result * levels(stream_key, dims, cuts, -0.22, 0.18)
    return jnp.clip(result, -reach, reach).astype(kind)


def setup_inputs(seed: int = 0) -> dict:
    arg_keys = jax.random.split(jax.random.key(seed), 10)
    return {
        "patches": noise(arg_keys[0], (PATCHES, D_V), 1.0, 6.0, ((0, 32),)),
        "vit_gain": jnp.clip(1.0 + 0.1 * jax.random.normal(arg_keys[1], (D_V,), jnp.float32), 0.5, 1.5),
        "fc_in": noise(arg_keys[2], (D_V, FF_V), D_V ** -0.5, 0.15625, ((1, 8),)),
        "fc_out": noise(arg_keys[3], (FF_V, D_V), FF_V ** -0.5, 0.078125, ((0, 8),)),
        "merge_gain": jnp.clip(1.0 + 0.1 * jax.random.normal(arg_keys[4], (D_V,), jnp.float32), 0.5, 1.5),
        "merge_shift": noise(arg_keys[5], (D_V,), 0.5, 3.0, (), jnp.float32),
        "merger": noise(arg_keys[6], (MERGED, D_L), MERGED ** -0.5, 0.078125, ((0, 32), (1, 8))),
        "counts": draw_counts(jax.random.fold_in(arg_keys[9], 71), 0),
        "grad_packed": noise(arg_keys[8], (N_DP * RECV, D_L), 1.0, 6.0, ((0, 32), (1, 8))),
    }


epsilon = 1e-06

def layer_norm(values, gain, shift):
    average = lax.optimization_barrier(jnp.mean(values, axis=-1, keepdims=True))
    centered = values - average
    variance = lax.optimization_barrier(jnp.mean(centered * centered, axis=-1, keepdims=True))
    return centered * lax.rsqrt(variance + epsilon) * gain + shift

def quick_gelu(values):
    return values * jax.nn.sigmoid(1.702 * values)

def reference(patches, vit_gain, fc_in, fc_out, merge_gain, merge_shift, merger, counts, grad_packed):
    inputs = patches.astype(jnp.float32)
    normed = layer_norm(inputs, vit_gain, 0.0).astype(jnp.bfloat16)
    block_hidden = FF_V // N_TENSOR
    layer_out = inputs
    for shard in range(N_TENSOR):
        hidden = quick_gelu(jnp.dot(normed, fc_in[:, shard * block_hidden:(shard + 1) * block_hidden], preferred_element_type=jnp.float32)).astype(jnp.bfloat16)
        term = jnp.dot(hidden, fc_out[shard * block_hidden:(shard + 1) * block_hidden, :], preferred_element_type=jnp.float32)
        layer_out = layer_out + term.astype(jnp.bfloat16).astype(jnp.float32)
    merged = layer_norm(layer_out, merge_gain, merge_shift).astype(jnp.bfloat16).reshape(TOKENS, MERGED)
    projected = jnp.dot(merged, merger, preferred_element_type=jnp.float32).astype(jnp.bfloat16)
    send_start = (jnp.cumsum(counts, axis=1) - counts).astype(jnp.int32)
    recv_start = (jnp.cumsum(counts, axis=0) - counts).astype(jnp.int32)
    recv_end = recv_start + counts
    position = jnp.arange(RECV, dtype=jnp.int32)
    owners = jnp.arange(N_DP, dtype=jnp.int32)
    source = lax.optimization_barrier(jnp.sum((recv_end[:, :, None] <= position[None, None, :]).astype(jnp.int32), axis=0))
    source = jnp.minimum(source, N_DP - 1).astype(jnp.int32)
    placed_valid = position[None, :] < lax.optimization_barrier(jnp.sum(counts, axis=0))[:, None]
    token_index = source * TOK_DEV + send_start[source, owners[:, None]] + position[None, :] - recv_start[source, owners[:, None]]
    token_index = jnp.clip(token_index, 0, TOKENS - 1).astype(jnp.int32)
    visual = jnp.where(placed_valid[:, :, None], projected[token_index], jnp.zeros((), jnp.bfloat16))
    visual = visual.reshape(N_DP * RECV, D_L).astype(jnp.bfloat16)
    local = jnp.arange(TOK_DEV, dtype=jnp.int32)
    senders = jnp.arange(N_DP, dtype=jnp.int32)
    send_end = send_start + counts
    target = lax.optimization_barrier(jnp.sum((send_end[:, :, None] <= local[None, None, :]).astype(jnp.int32), axis=1))
    target = jnp.minimum(target, N_DP - 1).astype(jnp.int32)
    packed_row = target * RECV + recv_start[senders[:, None], target] + local[None, :] - send_start[senders[:, None], target]
    token_grads = grad_packed[packed_row.reshape(TOKENS).astype(jnp.int32)]
    grad_scale = 1.0 / math.sqrt(TOKENS)

    def add_term(index, total):
        rows_part = lax.dynamic_slice_in_dim(merged, index * TOK_DEV, TOK_DEV, 0)
        grads_part = lax.dynamic_slice_in_dim(token_grads, index * TOK_DEV, TOK_DEV, 0)
        term = lax.dot_general(rows_part, grads_part, (((0,), (0,)), ((), ())), preferred_element_type=jnp.float32) * grad_scale
        return total + term.astype(jnp.bfloat16).astype(jnp.float32)
    grad_weight = lax.fori_loop(0, N_DP, add_term, jnp.zeros((MERGED, D_L), jnp.float32))
    block_model = D_L // N_TENSOR
    merged_grads = jnp.zeros((TOKENS, MERGED), jnp.float32)
    for shard in range(N_TENSOR):
        term = lax.dot_general(token_grads[:, shard * block_model:(shard + 1) * block_model], merger[:, shard * block_model:(shard + 1) * block_model], (((1,), (1,)), ((), ())), preferred_element_type=jnp.float32)
        merged_grads = merged_grads + term.astype(jnp.bfloat16).astype(jnp.float32)
    merged_grads = merged_grads.reshape(PATCHES, D_V)
    average = lax.optimization_barrier(jnp.mean(layer_out, axis=-1, keepdims=True))
    centered = layer_out - average
    inverse = lax.rsqrt(lax.optimization_barrier(jnp.mean(centered * centered, axis=-1, keepdims=True)) + epsilon)
    normal = centered * inverse
    scaled = merged_grads * merge_gain
    grad_layer = inverse * (scaled - lax.optimization_barrier(jnp.mean(scaled, axis=-1, keepdims=True)) - normal * lax.optimization_barrier(jnp.mean(scaled * normal, axis=-1, keepdims=True)))
    return (visual, grad_weight, grad_layer)
```

```python
import math

import jax
import jax.numpy as jnp
from jax import lax
from jax.sharding import Mesh
from jax.sharding import PartitionSpec as P

epsilon = 1e-06
bf16 = jnp.bfloat16
f32 = jnp.float32
DP = ("x", "y", "c")
SWAP = [(0, 1), (1, 0)]


def layer_norm(values, gain, shift):
    average = jnp.mean(values, axis=-1, keepdims=True)
    centered = values - average
    variance = jnp.mean(centered * centered, axis=-1, keepdims=True)
    return centered * lax.rsqrt(variance + epsilon) * gain + shift


def quick_gelu(values):
    return values * jax.nn.sigmoid(1.702 * values)


def exclusive_sum(values):
    return jnp.cumsum(values) - values


def position(x, y, c):
    return ((x % 4) * 4 + (y % 4)) * 2 + c


def ring_pairs(axis):
    pairs = []
    for x in range(4):
        for y in range(4):
            for c in range(2):
                step = 1 - 2 * c
                to = position(x + step, y, c) if axis == "x" else position(x, y + step, c)
                pairs.append((position(x, y, c), to))
    return pairs


def pick(array, index, axis):
    return lax.dynamic_index_in_dim(array, index % 4, axis, keepdims=False)


def scatter_chips(parts):
    place = {"x": lax.axis_index("x"), "y": lax.axis_index("y")}
    sign = 1 - 2 * lax.axis_index("c")
    dim = {"x": 0, "y": 1}
    pairs = {"x": ring_pairs("x"), "y": ring_pairs("y")}
    running = [pick(a, place[ax] - sign, dim[ax]) for ax, a in parts]
    for step in range(3):
        for i, (ax, a) in enumerate(parts):
            came = lax.ppermute(running[i], DP, pairs[ax])
            mine = pick(a, place[ax] - sign * (2 + step), dim[ax])
            running[i] = (came.astype(f32) + mine.astype(f32)).astype(bf16)
    sums = []
    for i, (ax, _) in enumerate(parts):
        other = "y" if ax == "x" else "x"
        total = pick(running[i], place[other], 0).astype(f32)
        for k in (1, 3, 2):
            block = pick(running[i], place[other] + k, 0)
            came = lax.ppermute(block, other, [(j, (j + k) % 4) for j in range(4)])
            total = total + came.astype(f32)
        sums.append(total)
    return sums


def body(patches, vit_gain, fc_in, fc_out, merge_gain, merge_shift, merger, counts, grad_packed):
    core = lax.axis_index("c")
    chip = lax.axis_index("x") * 4 + lax.axis_index("y")
    me = chip * 2 + core
    z = lax.axis_index("z")

    halves = merger.reshape(160, 2, 512)
    kept = lax.dynamic_index_in_dim(halves, core, 1, keepdims=False)
    given = lax.dynamic_index_in_dim(halves, 1 - core, 1, keepdims=False)
    got = lax.ppermute(given, "c", SWAP)
    both = jnp.where(core == 0, jnp.concatenate([kept, got]), jnp.concatenate([got, kept]))
    weight = lax.all_gather(both, ("x", "y"), axis=0, tiled=True)

    inputs = patches.astype(f32)
    normed = layer_norm(inputs, vit_gain, 0.0).astype(bf16)
    hidden = quick_gelu(jnp.dot(normed, fc_in, preferred_element_type=f32)).astype(bf16)
    summed = lax.psum_scatter(
        jnp.dot(hidden, fc_out, preferred_element_type=f32).astype(bf16),
        "z",
        scatter_dimension=0,
        tiled=True,
    ).astype(f32)

    slot = jnp.arange(16, dtype=jnp.int32)
    recv_counts = lax.dynamic_index_in_dim(counts, me, 1, keepdims=False)
    recv_start = exclusive_sum(recv_counts)
    packed_row = jnp.where(
        slot[None, :] < recv_counts[:, None], recv_start[:, None] + slot[None, :], -1
    ).reshape(512)
    pack = (packed_row[:, None] == jnp.arange(512, dtype=jnp.int32)[None, :]).astype(bf16)
    send_counts = lax.dynamic_slice_in_dim(counts, chip * 2, 2, 0)
    send_start = jnp.cumsum(send_counts, axis=1) - send_counts
    first = send_start.T[:, :, None] + slot + 256 * jnp.arange(2, dtype=jnp.int32)[None, :, None]
    token = jnp.where(slot < send_counts.T[:, :, None], first, -1).reshape(1024)
    route = (jnp.arange(512, dtype=jnp.int32)[:, None] == token[None, :]).astype(bf16)

    returning = jnp.stack(
        [
            jnp.dot(pack, grad_packed[:, :512], preferred_element_type=f32).astype(bf16).reshape(16, 32, 512),
            jnp.dot(pack, grad_packed[:, 512:], preferred_element_type=f32).astype(bf16).reshape(16, 32, 512),
        ],
        axis=1,
    ).reshape(32, 32, 512)
    arrived = lax.all_to_all(returning, DP, split_axis=0, concat_axis=0, tiled=True)
    token_grads = jnp.dot(
        route, arrived.reshape(1024, 512), preferred_element_type=f32
    ).astype(bf16)

    layer_out = lax.dynamic_slice_in_dim(inputs, z * 128, 128, 0) + summed
    average = jnp.mean(layer_out, axis=-1, keepdims=True)
    centered = layer_out - average
    inverse = lax.rsqrt(jnp.mean(centered * centered, axis=-1, keepdims=True) + epsilon)
    normal = centered * inverse
    normed_mine = (normal * merge_gain + merge_shift).astype(bf16)
    merged_own = lax.all_gather(normed_mine.reshape(32, 5120), "z", axis=0, tiled=True)
    merged_other = lax.ppermute(merged_own, "c", SWAP)
    merged = jnp.where(
        core == 0,
        jnp.concatenate([merged_own, merged_other]),
        jnp.concatenate([merged_other, merged_own]),
    )

    scale = 1.0 / math.sqrt(8192)
    parts = []
    for i, ax in enumerate("xy"):
        part = lax.dot_general(
            merged,
            token_grads[:, 256 * i : 256 * (i + 1)],
            (((0,), (0,)), ((), ())),
            preferred_element_type=f32,
        )
        parts.append((ax, (part * scale).astype(bf16).reshape(4, 4, 320, 256)))
    sums = scatter_chips(parts)
    chip_rows = jnp.concatenate(sums, axis=1).reshape(2, 160, 512)
    mine = lax.dynamic_index_in_dim(chip_rows, core, 0, keepdims=False)
    other = lax.ppermute(
        lax.dynamic_index_in_dim(chip_rows, 1 - core, 0, keepdims=False), "c", SWAP
    )
    grad_weight = jnp.where(
        core == 0,
        jnp.concatenate([mine, other], axis=1),
        jnp.concatenate([other, mine], axis=1),
    )

    projected = jnp.dot(merged, weight, preferred_element_type=f32).astype(bf16)
    outgoing = lax.dot_general(
        route, projected, (((0,), (0,)), ((), ())), preferred_element_type=f32
    ).astype(bf16)
    incoming = lax.all_to_all(
        outgoing.reshape(32, 32, 512), DP, split_axis=0, concat_axis=0, tiled=True
    ).reshape(16, 2, 512 // 16, 512)
    visual = jnp.concatenate(
        [
            lax.dot_general(
                pack,
                incoming[:, h].reshape(512, 512),
                (((0,), (0,)), ((), ())),
                preferred_element_type=f32,
            ).astype(bf16)
            for h in range(2)
        ],
        axis=1,
    )

    partial = lax.dot_general(
        token_grads, weight, (((1,), (1,)), ((), ())), preferred_element_type=f32
    ).astype(bf16).reshape(2, 256, 5120)
    kept = lax.dynamic_index_in_dim(partial, core, 0, keepdims=False)
    given = lax.dynamic_index_in_dim(partial, 1 - core, 0, keepdims=False)
    chip_grads = (kept.astype(f32) + lax.ppermute(given, "c", SWAP).astype(f32)).astype(bf16)
    merged_grads = (
        lax.psum_scatter(chip_grads, "z", scatter_dimension=0, tiled=True)
        .astype(f32)
        .reshape(128, 1280)
    )
    scaled = merged_grads * merge_gain
    grad_layer = inverse * (
        scaled
        - jnp.mean(scaled, axis=-1, keepdims=True)
        - normal * jnp.mean(scaled * normal, axis=-1, keepdims=True)
    )
    return (visual, grad_weight, grad_layer)


def solution(mesh):
    grid = Mesh(mesh.devices.reshape(4, 4, 2, 8), ("x", "y", "c", "z"))
    in_specs = (
        P(DP, None),
        P(),
        P(None, "z"),
        P("z", None),
        P(),
        P(),
        P(DP, "z"),
        P(),
        P(DP, "z"),
    )
    out_specs = (P(DP, "z"), P(DP, "z"), P((*DP, "z"), None))
    return jax.shard_map(body, mesh=grid, in_specs=in_specs, out_specs=out_specs, check_vma=False)
```

```python
import math

import jax
import jax.numpy as jnp
from jax import lax
from jax.sharding import Mesh
from jax.sharding import PartitionSpec as P

epsilon = 1e-06
bf16 = jnp.bfloat16
f32 = jnp.float32
DP = ("x", "y", "c")
SWAP = [(0, 1), (1, 0)]


def layer_norm(values, gain, shift):
    average = jnp.mean(values, axis=-1, keepdims=True)
    centered = values - average
    variance = jnp.mean(centered * centered, axis=-1, keepdims=True)
    return centered * lax.rsqrt(variance + epsilon) * gain + shift


def quick_gelu(values):
    return values * jax.nn.sigmoid(1.702 * values)


def exclusive_sum(values):
    return jnp.cumsum(values) - values


def position(x, y, c):
    return ((x % 4) * 4 + (y % 4)) * 2 + c


def ring_pairs(axis):
    pairs = []
    for x in range(4):
        for y in range(4):
            for c in range(2):
                step = 1 - 2 * c
                to = position(x + step, y, c) if axis == "x" else position(x, y + step, c)
                pairs.append((position(x, y, c), to))
    return pairs


def pick(array, index, axis):
    return lax.dynamic_index_in_dim(array, index % 4, axis, keepdims=False)


def scatter_chips(parts):
    place = {"x": lax.axis_index("x"), "y": lax.axis_index("y")}
    sign = 1 - 2 * lax.axis_index("c")
    dim = {"x": 0, "y": 1}
    pairs = {"x": ring_pairs("x"), "y": ring_pairs("y")}
    running = [pick(a, place[ax] - sign, dim[ax]) for ax, a in parts]
    for step in range(3):
        for i, (ax, a) in enumerate(parts):
            came = lax.ppermute(running[i], DP, pairs[ax])
            mine = pick(a, place[ax] - sign * (2 + step), dim[ax])
            running[i] = (came.astype(f32) + mine.astype(f32)).astype(bf16)
    sums = []
    for i, (ax, _) in enumerate(parts):
        other = "y" if ax == "x" else "x"
        total = pick(running[i], place[other], 0).astype(f32)
        for k in (1, 3, 2):
            block = pick(running[i], place[other] + k, 0)
            came = lax.ppermute(block, other, [(j, (j + k) % 4) for j in range(4)])
            total = total + came.astype(f32)
        sums.append(total)
    return sums


def body(patches, vit_gain, fc_in, fc_out, merge_gain, merge_shift, merger, counts, grad_packed):
    core = lax.axis_index("c")
    chip = lax.axis_index("x") * 4 + lax.axis_index("y")
    me = chip * 2 + core
    z = lax.axis_index("z")

    halves = merger.reshape(160, 2, 512)
    kept = lax.dynamic_index_in_dim(halves, core, 1, keepdims=False)
    given = lax.dynamic_index_in_dim(halves, 1 - core, 1, keepdims=False)
    got = lax.ppermute(given, "c", SWAP)
    both = jnp.where(core == 0, jnp.concatenate([kept, got]), jnp.concatenate([got, kept]))
    weight = lax.all_gather(both, ("x", "y"), axis=0, tiled=True)

    inputs = patches.astype(f32)
    normed = layer_norm(inputs, vit_gain, 0.0).astype(bf16)
    hidden = quick_gelu(jnp.dot(normed, fc_in, preferred_element_type=f32)).astype(bf16)
    summed = lax.psum_scatter(
        jnp.dot(hidden, fc_out, preferred_element_type=f32).astype(bf16),
        "z",
        scatter_dimension=0,
        tiled=True,
    ).astype(f32)

    slot = jnp.arange(16, dtype=jnp.int32)
    recv_counts = lax.dynamic_index_in_dim(counts, me, 1, keepdims=False)
    recv_start = exclusive_sum(recv_counts)
    packed_row = jnp.where(
        slot[None, :] < recv_counts[:, None], recv_start[:, None] + slot[None, :], -1
    ).reshape(512)
    pack = (packed_row[:, None] == jnp.arange(512, dtype=jnp.int32)[None, :]).astype(bf16)
    send_counts = lax.dynamic_slice_in_dim(counts, chip * 2, 2, 0)
    send_start = jnp.cumsum(send_counts, axis=1) - send_counts
    base = 256 * (jnp.arange(2, dtype=jnp.int32) ^ core)
    first = send_start.T[:, :, None] + slot + base[None, :, None]
    token = jnp.where(slot < send_counts.T[:, :, None], first, -1).reshape(1024)
    route = (jnp.arange(512, dtype=jnp.int32)[:, None] == token[None, :]).astype(bf16)

    returning = jnp.stack(
        [
            jnp.dot(pack, grad_packed[:, :512], preferred_element_type=f32).astype(bf16).reshape(16, 32, 512),
            jnp.dot(pack, grad_packed[:, 512:], preferred_element_type=f32).astype(bf16).reshape(16, 32, 512),
        ],
        axis=1,
    ).reshape(32, 32, 512)
    arrived = lax.all_to_all(returning, DP, split_axis=0, concat_axis=0, tiled=True)
    token_grads = jnp.dot(
        route, arrived.reshape(1024, 512), preferred_element_type=f32
    ).astype(bf16)

    layer_out = lax.dynamic_slice_in_dim(inputs, z * 128, 128, 0) + summed
    average = jnp.mean(layer_out, axis=-1, keepdims=True)
    centered = layer_out - average
    inverse = lax.rsqrt(jnp.mean(centered * centered, axis=-1, keepdims=True) + epsilon)
    normal = centered * inverse
    normed_mine = (normal * merge_gain + merge_shift).astype(bf16)
    merged_own = lax.all_gather(normed_mine.reshape(32, 5120), "z", axis=0, tiled=True)
    merged_other = lax.ppermute(merged_own, "c", SWAP)
    merged = jnp.concatenate([merged_own, merged_other])

    scale = 1.0 / math.sqrt(8192)
    parts = []
    for i, ax in enumerate("xy"):
        part = lax.dot_general(
            merged,
            token_grads[:, 256 * i : 256 * (i + 1)],
            (((0,), (0,)), ((), ())),
            preferred_element_type=f32,
        )
        parts.append((ax, (part * scale).astype(bf16).reshape(4, 4, 320, 256)))
    sums = scatter_chips(parts)
    chip_rows = jnp.concatenate(sums, axis=1).reshape(2, 160, 512)
    mine = lax.dynamic_index_in_dim(chip_rows, core, 0, keepdims=False)
    other = lax.ppermute(
        lax.dynamic_index_in_dim(chip_rows, 1 - core, 0, keepdims=False), "c", SWAP
    )
    grad_weight = jnp.where(
        core == 0,
        jnp.concatenate([mine, other], axis=1),
        jnp.concatenate([other, mine], axis=1),
    )

    projected = jnp.dot(merged, weight, preferred_element_type=f32).astype(bf16)
    outgoing = lax.dot_general(
        route, projected, (((0,), (0,)), ((), ())), preferred_element_type=f32
    ).astype(bf16)
    incoming = lax.all_to_all(
        outgoing.reshape(32, 32, 512), DP, split_axis=0, concat_axis=0, tiled=True
    ).reshape(16, 2, 512 // 16, 512)
    visual = jnp.concatenate(
        [
            lax.dot_general(
                pack,
                incoming[:, h].reshape(512, 512),
                (((0,), (0,)), ((), ())),
                preferred_element_type=f32,
            ).astype(bf16)
            for h in range(2)
        ],
        axis=1,
    )

    held_grads, _ = lax.optimization_barrier((token_grads, normed_mine))
    partial = lax.dot_general(
        held_grads, weight, (((1,), (1,)), ((), ())), preferred_element_type=f32
    ).astype(bf16)
    chip_grads = (
        partial[:256].astype(f32) + lax.ppermute(partial[256:], "c", SWAP).astype(f32)
    ).astype(bf16)
    merged_grads = (
        lax.psum_scatter(chip_grads, "z", scatter_dimension=0, tiled=True)
        .astype(f32)
        .reshape(128, 1280)
    )
    scaled = merged_grads * merge_gain
    grad_layer = inverse * (
        scaled
        - jnp.mean(scaled, axis=-1, keepdims=True)
        - normal * jnp.mean(scaled * normal, axis=-1, keepdims=True)
    )
    return (visual, grad_weight, grad_layer)


def solution(mesh):
    grid = Mesh(mesh.devices.reshape(4, 4, 2, 8), ("x", "y", "c", "z"))
    in_specs = (
        P(DP, None),
        P(),
        P(None, "z"),
        P("z", None),
        P(),
        P(),
        P(DP, "z"),
        P(),
        P(DP, "z"),
    )
    out_specs = (P(DP, "z"), P(DP, "z"), P((*DP, "z"), None))
    return jax.shard_map(body, mesh=grid, in_specs=in_specs, out_specs=out_specs, check_vma=False)
```

```python
import functools
import math

import jax
import jax.numpy as jnp
from jax import lax
from jax.experimental import pallas as pl
from jax.experimental.pallas import tpu as pltpu
from jax.sharding import Mesh
from jax.sharding import PartitionSpec as P

epsilon = 1e-06
bf16 = jnp.bfloat16
f32 = jnp.float32
DP = ("x", "y", "c")
SWAP = [(0, 1), (1, 0)]


def layer_norm(values, gain, shift):
    average = jnp.mean(values, axis=-1, keepdims=True)
    centered = values - average
    variance = jnp.mean(centered * centered, axis=-1, keepdims=True)
    return centered * lax.rsqrt(variance + epsilon) * gain + shift


def quick_gelu(values):
    return values * jax.nn.sigmoid(1.702 * values)


def exclusive_sum(values):
    return jnp.cumsum(values) - values


def position(x, y, c):
    return ((x % 4) * 4 + (y % 4)) * 2 + c


def ring_pairs(axis):
    pairs = []
    for x in range(4):
        for y in range(4):
            for c in range(2):
                step = 1 - 2 * c
                to = position(x + step, y, c) if axis == "x" else position(x, y + step, c)
                pairs.append((position(x, y, c), to))
    return pairs


def pick(array, index, axis):
    return lax.dynamic_index_in_dim(array, index % 4, axis, keepdims=False)


def pick_core(array, core):
    return lax.dynamic_index_in_dim(array, core, 0, keepdims=False)


def gather_lines(block):
    place = {"x": lax.axis_index("x"), "y": lax.axis_index("y")}
    sign = 1 - 2 * lax.axis_index("c")
    lines = []
    for i, first in enumerate("yx"):
        mine = block[:, 256 * i : 256 * (i + 1)]
        line = jnp.broadcast_to(mine, (4, 320, 256))
        for k in (1, 3, 2):
            came = lax.ppermute(mine, first, [((j + k) % 4, j) for j in range(4)])
            line = lax.dynamic_update_index_in_dim(line, came, (place[first] + k) % 4, 0)
        lines.append(line)
    return lines


def gather_chips(held, after):
    place = {"x": lax.axis_index("x"), "y": lax.axis_index("y")}
    sign = 1 - 2 * lax.axis_index("c")
    pairs = {"x": ring_pairs("x"), "y": ring_pairs("y")}
    whole = jnp.zeros((4, 4, 320, 512), bf16)
    for step in range(4):
        if step == 2:
            held, after = lax.optimization_barrier((held, after))
        for i, ring in enumerate("xy"):
            if step:
                held[i] = lax.ppermute(held[i], DP, pairs[ring])
            at = (place[ring] - sign * step) % 4
            if ring == "x":
                whole = lax.dynamic_update_slice(whole, held[i][None], (at, 0, 0, 256 * i))
            else:
                whole = lax.dynamic_update_slice(whole, held[i][:, None], (0, at, 0, 256 * i))
    return whole.reshape(5120, 512), after


def product(tokens, grads, scale):
    total = lax.dot_general(tokens, grads, (((0,), (0,)), ((), ())), preferred_element_type=f32)
    return (total * scale).astype(bf16)


def first_kernel(scale, order, tokens, grads, a0, b0, b1, b2, b3, held):
    @pl.when(pl.program_id(0) == 0)
    def _():
        a0[...] = product(tokens[...], grads[:, :256], scale)

    held[...] = product(tokens[...], grads[:, 256:], scale)
    for m, b in enumerate((b0, b1, b2, b3)):
        b[0] = held[pl.ds(pl.multiple_of(order[4 + m] * 320, 64), 320), :]


def rest_kernel(scale, order, tokens, grads, *rest):
    for k, a in enumerate(rest):

        @pl.when(pl.program_id(0) == k)
        def _():
            a[...] = product(tokens[...], grads[:, :256], scale)


def weight_blocks(tokens, grads, later, scale):
    place = [lax.axis_index("x"), lax.axis_index("y")]
    sign = 1 - 2 * lax.axis_index("c")
    order = jnp.stack([(p - sign * k) % 4 for p in place for k in (1, 2, 3, 4)]).astype(jnp.int32)
    params = pltpu.CompilerParams(vmem_limit_bytes=60 * 2**20)
    flat = jax.ShapeDtypeStruct((1280, 256), bf16)
    deep = jax.ShapeDtypeStruct((4, 320, 256), bf16)
    whole = pl.BlockSpec((1280, 256), lambda k, o: (0, 0))
    a0, *deeps = pl.pallas_call(
        functools.partial(first_kernel, scale),
        out_shape=[flat] + [deep] * 4,
        grid_spec=pltpu.PrefetchScalarGridSpec(
            num_scalar_prefetch=1,
            grid=(4,),
            in_specs=[
                pl.BlockSpec((512, 1280), lambda k, o: (0, o[k])),
                pl.BlockSpec((512, 512), lambda k, o: (0, 0)),
            ],
            out_specs=[whole] + [pl.BlockSpec((1, 320, 256), lambda k, o: (o[k], 0, 0))] * 4,
            scratch_shapes=[pltpu.VMEM((1280, 256), bf16)],
        ),
        compiler_params=params,
        cost_estimate=pl.CostEstimate(flops=10 * 512 * 1280 * 256, bytes_accessed=9 * 2**20, transcendentals=0),
        name="weight_first",
    )(order, tokens, grads)
    a0, grads, later = lax.optimization_barrier((a0, grads, later))
    rest = pl.pallas_call(
        functools.partial(rest_kernel, scale),
        out_shape=[flat] * 3,
        grid_spec=pltpu.PrefetchScalarGridSpec(
            num_scalar_prefetch=1,
            grid=(3,),
            in_specs=[
                pl.BlockSpec((512, 1280), lambda k, o: (0, o[k + 1])),
                pl.BlockSpec((512, 512), lambda k, o: (0, 0)),
            ],
            out_specs=[whole] * 3,
        ),
        compiler_params=params,
        cost_estimate=pl.CostEstimate(flops=6 * 512 * 1280 * 256, bytes_accessed=7 * 2**20, transcendentals=0),
        name="weight_rest",
    )(order, tokens, grads)
    return [a.reshape(4, 320, 256) for a in (a0, *rest)], deeps, later


def scatter_chips(blocks, later):
    place = {"x": lax.axis_index("x"), "y": lax.axis_index("y")}
    parts = list(zip("xy", blocks))
    pairs = {"x": ring_pairs("x"), "y": ring_pairs("y")}
    running = [a[0] for _, a in parts]
    for step in range(3):
        if step == 2:
            running, later = lax.optimization_barrier((running, later))
        for i, (ax, a) in enumerate(parts):
            came = lax.ppermute(running[i], DP, pairs[ax])
            running[i] = (came.astype(f32) + a[step + 1].astype(f32)).astype(bf16)
    return running, later


def exchange_chips(running, earlier):
    place = {"x": lax.axis_index("x"), "y": lax.axis_index("y")}
    sums = []
    for line, other in zip(running, "yx"):
        terms = [pick(line, place[other], 0)]
        for k in (1, 3, 2):
            block = pick(line, place[other] + k, 0)
            terms.append(lax.ppermute(block, other, [(j, (j + k) % 4) for j in range(4)]))
        if other == "x":
            terms, earlier = lax.optimization_barrier((terms, earlier))
        sums.append(sum(t.astype(f32) for t in terms))
    return sums, earlier


def body(patches, vit_gain, fc_in, fc_out, merge_gain, merge_shift, merger, counts, grad_packed):
    core = lax.axis_index("c")
    chip = lax.axis_index("x") * 4 + lax.axis_index("y")
    me = chip * 2 + core
    z = lax.axis_index("z")

    halves = merger.reshape(160, 2, 512)
    kept = lax.dynamic_index_in_dim(halves, core, 1, keepdims=False)
    given = lax.dynamic_index_in_dim(halves, 1 - core, 1, keepdims=False)
    got = lax.ppermute(given, "c", SWAP)
    both = jnp.where(core == 0, jnp.concatenate([kept, got]), jnp.concatenate([got, kept]))
    lines = gather_lines(both)

    inputs = patches.astype(f32)
    normed = layer_norm(inputs, vit_gain, 0.0).astype(bf16)
    hidden = quick_gelu(jnp.dot(normed, fc_in, preferred_element_type=f32)).astype(bf16)
    summed = lax.psum_scatter(
        jnp.dot(hidden, fc_out, preferred_element_type=f32).astype(bf16),
        "z",
        scatter_dimension=0,
        tiled=True,
    )

    slot = jnp.arange(16, dtype=jnp.int32)
    recv_counts = lax.dynamic_index_in_dim(counts, me, 1, keepdims=False)
    recv_start = exclusive_sum(recv_counts)
    packed_row = jnp.where(
        slot[None, :] < recv_counts[:, None], recv_start[:, None] + slot[None, :], -1
    ).reshape(512)
    pack = (packed_row[:, None] == jnp.arange(512, dtype=jnp.int32)[None, :]).astype(bf16)
    send_counts = lax.dynamic_slice_in_dim(counts, chip * 2, 2, 0)
    send_start = jnp.cumsum(send_counts, axis=1) - send_counts
    base = 256 * jnp.arange(2, dtype=jnp.int32)
    first = send_start.T[:, :, None] + slot + base[None, :, None]
    token = jnp.where(slot < send_counts.T[:, :, None], first, -1).reshape(1024)
    route = (jnp.arange(512, dtype=jnp.int32)[:, None] == token[None, :]).astype(bf16)

    returning = jnp.stack(
        [
            jnp.dot(pack, grad_packed[:, :512], preferred_element_type=f32).astype(bf16).reshape(16, 32, 512),
            jnp.dot(pack, grad_packed[:, 512:], preferred_element_type=f32).astype(bf16).reshape(16, 32, 512),
        ],
        axis=1,
    ).reshape(32, 32, 512)
    arrived = lax.all_to_all(returning, DP, split_axis=0, concat_axis=0, tiled=True)
    summed, arrived = lax.optimization_barrier((summed, arrived))
    token_grads = jnp.dot(
        route, arrived.reshape(1024, 512), preferred_element_type=f32
    ).astype(bf16)

    mine = lax.dynamic_slice_in_dim(patches, z * 128, 128, 0)
    layer_out = mine.astype(f32) + summed.astype(f32)
    average = jnp.mean(layer_out, axis=-1, keepdims=True)
    centered = layer_out - average
    inverse = lax.rsqrt(jnp.mean(centered * centered, axis=-1, keepdims=True) + epsilon)
    normal = centered * inverse
    normed_mine = (normal * merge_gain + merge_shift).astype(bf16)
    weight, normed_mine = gather_chips(lines, normed_mine)
    merged = lax.all_gather(normed_mine.reshape(32, 5120), ("c", "z"), axis=0, tiled=True)

    def back(grads):
        return lax.dot_general(
            grads, weight, (((1,), (1,)), ((), ())), preferred_element_type=f32
        ).astype(bf16)

    by_core = token_grads.reshape(2, 256, 512)
    given = lax.ppermute(back(pick_core(by_core, 1 - core)), "c", SWAP)
    chip_grads = (back(pick_core(by_core, core)).astype(f32) + given.astype(f32)).astype(bf16)

    projected = jnp.dot(merged, weight, preferred_element_type=f32).astype(bf16)
    outgoing = lax.dot_general(
        route, projected, (((0,), (0,)), ((), ())), preferred_element_type=f32
    ).astype(bf16)

    first_x, first_y, chip_grads = weight_blocks(
        merged, token_grads, chip_grads, 1.0 / math.sqrt(8192)
    )
    running, outgoing = scatter_chips((first_x, first_y), outgoing)
    incoming = lax.all_to_all(
        outgoing.reshape(32, 32, 512), DP, split_axis=0, concat_axis=0, tiled=True
    ).reshape(16, 2, 512 // 16, 512)
    visual = jnp.concatenate(
        [
            lax.dot_general(
                pack,
                incoming[:, h].reshape(512, 512),
                (((0,), (0,)), ((), ())),
                preferred_element_type=f32,
            ).astype(bf16)
            for h in range(2)
        ],
        axis=1,
    )

    merged_grads = (
        lax.psum_scatter(chip_grads, "z", scatter_dimension=0, tiled=True)
        .astype(f32)
        .reshape(128, 1280)
    )
    scaled = merged_grads * merge_gain
    grad_layer = inverse * (
        scaled
        - jnp.mean(scaled, axis=-1, keepdims=True)
        - normal * jnp.mean(scaled * normal, axis=-1, keepdims=True)
    )

    sums, grad_layer = exchange_chips(running, grad_layer)
    chip_rows = jnp.concatenate(sums, axis=1).reshape(2, 160, 512)
    mine = lax.dynamic_index_in_dim(chip_rows, core, 0, keepdims=False)
    other = lax.ppermute(
        lax.dynamic_index_in_dim(chip_rows, 1 - core, 0, keepdims=False), "c", SWAP
    )
    grad_weight = jnp.where(
        core == 0,
        jnp.concatenate([mine, other], axis=1),
        jnp.concatenate([other, mine], axis=1),
    )
    return (visual, grad_weight, grad_layer)


def solution(mesh):
    grid = Mesh(mesh.devices.reshape(4, 4, 2, 8), ("x", "y", "c", "z"))
    in_specs = (
        P(DP, None),
        P(),
        P(None, "z"),
        P("z", None),
        P(),
        P(),
        P(DP, "z"),
        P(),
        P(DP, "z"),
    )
    out_specs = (P(DP, "z"), P(DP, "z"), P((*DP, "z"), None))
    return jax.shard_map(body, mesh=grid, in_specs=in_specs, out_specs=out_specs, check_vma=False)
```

```python
import math

import jax
import jax.numpy as jnp
from jax import lax
from jax.experimental import pallas as pl
from jax.experimental.pallas import tpu as pltpu
from jax.sharding import Mesh
from jax.sharding import PartitionSpec as P

epsilon = 1e-06
bf16 = jnp.bfloat16
f32 = jnp.float32
DP = ("x", "y", "c")
SWAP = [(0, 1), (1, 0)]
VMEM = 60 * 2**20


def vision_kernel(patches, gain, fc_in, fc_out, out):
    for r in range(0, patches.shape[0], 256):
        values = patches[r : r + 256, :].astype(f32)
        centered = values - jnp.mean(values, axis=-1, keepdims=True)
        variance = jnp.mean(centered * centered, axis=-1, keepdims=True)
        normed = (centered * lax.rsqrt(variance + epsilon) * gain[...]).astype(bf16)
        hidden = jnp.dot(normed, fc_in[...], preferred_element_type=f32)
        hidden = (hidden * jax.nn.sigmoid(1.702 * hidden)).astype(bf16)
        term = jnp.dot(hidden, fc_out[...], preferred_element_type=f32)
        out[r : r + 256, :] = term.astype(bf16)


def vision(patches, gain, fc_in, fc_out):
    rows, width = patches.shape
    tile = pl.BlockSpec((512, width), lambda i: (i, 0))
    return pl.pallas_call(
        vision_kernel,
        out_shape=jax.ShapeDtypeStruct((rows, width), bf16),
        grid=(rows // 512,),
        in_specs=[tile, pl.BlockSpec((width,), lambda i: (0,))]
        + [pl.BlockSpec(a.shape, lambda i: (0, 0)) for a in (fc_in, fc_out)],
        out_specs=tile,
        compiler_params=pltpu.CompilerParams(vmem_limit_bytes=VMEM),
        cost_estimate=pl.CostEstimate(flops=4 * rows * width * 640, bytes_accessed=9 * 2**20, transcendentals=rows * 640),
        name="vision",
    )(patches, gain, fc_in, fc_out)


def norm_kernel(z, patches, summed, gain, shift, tokens, normal, inverse, held):
    layer_out = patches[...].astype(f32) + summed[...].astype(f32)
    centered = layer_out - jnp.mean(layer_out, axis=-1, keepdims=True)
    scale = lax.rsqrt(jnp.mean(centered * centered, axis=-1, keepdims=True) + epsilon)
    normal[...] = centered * scale
    inverse[...] = jnp.broadcast_to(scale, inverse.shape)
    held[...] = (normal[...] * gain[...] + shift[...]).reshape(held.shape)
    for j in range(4):
        tokens[:, 1280 * j : 1280 * (j + 1)] = held[:, j, :].astype(bf16)


def norm(z, patches, summed, gain, shift):
    fixed = lambda i, z: (0, 0)
    row = pl.BlockSpec((1280,), lambda i, z: (0,))
    return pl.pallas_call(
        norm_kernel,
        out_shape=[
            jax.ShapeDtypeStruct((32, 5120), bf16),
            jax.ShapeDtypeStruct((128, 1280), f32),
            jax.ShapeDtypeStruct((128, 128), f32),
        ],
        grid_spec=pltpu.PrefetchScalarGridSpec(
            num_scalar_prefetch=1,
            grid=(1,),
            in_specs=[
                pl.BlockSpec((128, 1280), lambda i, z: (z[0], 0)),
                pl.BlockSpec((128, 1280), fixed),
                row,
                row,
            ],
            out_specs=[
                pl.BlockSpec((32, 5120), fixed),
                pl.BlockSpec((128, 1280), fixed),
                pl.BlockSpec((128, 128), fixed),
            ],
            scratch_shapes=[pltpu.VMEM((32, 4, 1280), f32)],
        ),
        compiler_params=pltpu.CompilerParams(vmem_limit_bytes=VMEM),
        name="norm",
    )(z, patches, summed, gain, shift)


def grad_kernel(grads, normal, inverse, gain, out, held):
    for j in range(4):
        held[:, j, :] = grads[:, 1280 * j : 1280 * (j + 1)].astype(f32)
    scaled = held[...].reshape(128, 1280) * gain[...]
    unit = normal[...]
    inner = jnp.mean(scaled * unit, axis=-1, keepdims=True)
    out[...] = inverse[:, :1] * (scaled - jnp.mean(scaled, axis=-1, keepdims=True) - unit * inner)


def layer_grad(grads, normal, inverse, gain):
    return pl.pallas_call(
        grad_kernel,
        out_shape=jax.ShapeDtypeStruct((128, 1280), f32),
        scratch_shapes=[pltpu.VMEM((32, 4, 1280), f32)],
        compiler_params=pltpu.CompilerParams(vmem_limit_bytes=VMEM),
        name="layer_grad",
    )(grads, normal, inverse, gain)


def exclusive_sum(values):
    return jnp.cumsum(values) - values


def position(x, y, c):
    return ((x % 4) * 4 + (y % 4)) * 2 + c


def ring_pairs(axis):
    pairs = []
    for x in range(4):
        for y in range(4):
            for c in range(2):
                step = 1 - 2 * c
                to = position(x + step, y, c) if axis == "x" else position(x, y + step, c)
                pairs.append((position(x, y, c), to))
    return pairs


def pick(array, index, axis):
    return lax.dynamic_index_in_dim(array, index % 4, axis, keepdims=False)


def pick_core(array, core):
    return lax.dynamic_index_in_dim(array, core, 0, keepdims=False)


def gather_lines(block):
    place = {"x": lax.axis_index("x"), "y": lax.axis_index("y")}
    sign = 1 - 2 * lax.axis_index("c")
    lines = []
    for i, first in enumerate("yx"):
        mine = block[:, 256 * i : 256 * (i + 1)]
        line = jnp.broadcast_to(mine, (4, 320, 256))
        for k in (1, 3, 2):
            came = lax.ppermute(mine, first, [((j + k) % 4, j) for j in range(4)])
            line = lax.dynamic_update_index_in_dim(line, came, (place[first] + k) % 4, 0)
        lines.append(line)
    return lines


def gather_chips(held, after):
    place = {"x": lax.axis_index("x"), "y": lax.axis_index("y")}
    sign = 1 - 2 * lax.axis_index("c")
    pairs = {"x": ring_pairs("x"), "y": ring_pairs("y")}
    whole = jnp.zeros((4, 4, 320, 512), bf16)
    for step in range(4):
        if step == 2:
            held, after = lax.optimization_barrier((held, after))
        for i, ring in enumerate("xy"):
            if step:
                held[i] = lax.ppermute(held[i], DP, pairs[ring])
            at = (place[ring] - sign * step) % 4
            if ring == "x":
                whole = lax.dynamic_update_slice(whole, held[i][None], (at, 0, 0, 256 * i))
            else:
                whole = lax.dynamic_update_slice(whole, held[i][:, None], (0, at, 0, 256 * i))
    return whole.reshape(5120, 512), after


def weight_kernel(order, tokens, grads, a0, rest, b0, b1, b2, b3, held):
    total = lax.dot_general(
        tokens[...], grads[...], (((0,), (0,)), ((), ())), preferred_element_type=f32
    ).astype(bf16)

    @pl.when(pl.program_id(0) == 0)
    def _():
        a0[...] = total[:, :256]

    @pl.when(pl.program_id(0) > 0)
    def _():
        rest[0] = total[:, :256]

    held[...] = total[:, 256:]
    for m, b in enumerate((b0, b1, b2, b3)):
        b[0] = held[pl.ds(pl.multiple_of(order[4 + m] * 320, 64), 320), :]


def weight_blocks(tokens, grads, later):
    place = [lax.axis_index("x"), lax.axis_index("y")]
    sign = 1 - 2 * lax.axis_index("c")
    order = jnp.stack([(p - sign * k) % 4 for p in place for k in (1, 2, 3, 4)]).astype(jnp.int32)
    flat = jax.ShapeDtypeStruct((1280, 256), bf16)
    deep = jax.ShapeDtypeStruct((4, 320, 256), bf16)
    a0, rest, *deeps = pl.pallas_call(
        weight_kernel,
        out_shape=[flat, jax.ShapeDtypeStruct((3, 1280, 256), bf16)] + [deep] * 4,
        grid_spec=pltpu.PrefetchScalarGridSpec(
            num_scalar_prefetch=1,
            grid=(4,),
            in_specs=[
                pl.BlockSpec((512, 1280), lambda k, o: (0, o[k])),
                pl.BlockSpec((512, 512), lambda k, o: (0, 0)),
            ],
            out_specs=[
                pl.BlockSpec((1280, 256), lambda k, o: (0, 0)),
                pl.BlockSpec((1, 1280, 256), lambda k, o: (jnp.maximum(k - 1, 0), 0, 0)),
            ]
            + [pl.BlockSpec((1, 320, 256), lambda k, o: (o[k], 0, 0))] * 4,
            scratch_shapes=[pltpu.VMEM((1280, 256), bf16)],
        ),
        compiler_params=pltpu.CompilerParams(vmem_limit_bytes=VMEM),
        cost_estimate=pl.CostEstimate(flops=16 * 512 * 1280 * 256, bytes_accessed=11 * 2**20, transcendentals=0),
        name="weight_product",
    )(order, tokens, grads)
    a0, later = lax.optimization_barrier((a0, later))
    return [a.reshape(4, 320, 256) for a in (a0, *rest)], deeps, later


def scatter_chips(blocks, later):
    place = {"x": lax.axis_index("x"), "y": lax.axis_index("y")}
    parts = list(zip("xy", blocks))
    pairs = {"x": ring_pairs("x"), "y": ring_pairs("y")}
    running = [a[0] for _, a in parts]
    for step in range(3):
        if step == 2:
            running, later = lax.optimization_barrier((running, later))
        for i, (ax, a) in enumerate(parts):
            came = lax.ppermute(running[i], DP, pairs[ax])
            running[i] = (came.astype(f32) + a[step + 1].astype(f32)).astype(bf16)
    return running, later


def exchange_chips(running, earlier):
    place = {"x": lax.axis_index("x"), "y": lax.axis_index("y")}
    sums = []
    for line, other in zip(running, "yx"):
        terms = [pick(line, place[other], 0)]
        for k in (1, 3, 2):
            block = pick(line, place[other] + k, 0)
            terms.append(lax.ppermute(block, other, [(j, (j + k) % 4) for j in range(4)]))
        if other == "x":
            terms, earlier = lax.optimization_barrier((terms, earlier))
        sums.append(sum(t.astype(f32) for t in terms))
    return sums, earlier


def body(patches, vit_gain, fc_in, fc_out, merge_gain, merge_shift, merger, counts, grad_packed):
    core = lax.axis_index("c")
    chip = lax.axis_index("x") * 4 + lax.axis_index("y")
    me = chip * 2 + core
    z = lax.axis_index("z")

    halves = merger.reshape(160, 2, 512)
    kept = lax.dynamic_index_in_dim(halves, core, 1, keepdims=False)
    given = lax.dynamic_index_in_dim(halves, 1 - core, 1, keepdims=False)
    got = lax.ppermute(given, "c", SWAP)
    both = jnp.where(core == 0, jnp.concatenate([kept, got]), jnp.concatenate([got, kept]))
    lines = gather_lines(both)

    summed = lax.psum_scatter(
        vision(patches, vit_gain, fc_in, fc_out), "z", scatter_dimension=0, tiled=True
    )

    slot = jnp.arange(16, dtype=jnp.int32)
    recv_counts = lax.dynamic_index_in_dim(counts, me, 1, keepdims=False)
    recv_start = exclusive_sum(recv_counts)
    packed_row = jnp.where(
        slot[None, :] < recv_counts[:, None], recv_start[:, None] + slot[None, :], -1
    ).reshape(512)
    pack = (packed_row[:, None] == jnp.arange(512, dtype=jnp.int32)[None, :]).astype(bf16)
    send_counts = lax.dynamic_slice_in_dim(counts, chip * 2, 2, 0)
    send_start = jnp.cumsum(send_counts, axis=1) - send_counts
    base = 256 * jnp.arange(2, dtype=jnp.int32)
    first = send_start.T[:, :, None] + slot + base[None, :, None]
    token = jnp.where(slot < send_counts.T[:, :, None], first, -1).reshape(1024)
    route = (jnp.arange(512, dtype=jnp.int32)[:, None] == token[None, :]).astype(bf16)

    returning = jnp.stack(
        [
            jnp.dot(pack, grad_packed[:, :512], preferred_element_type=f32).astype(bf16).reshape(16, 32, 512),
            jnp.dot(pack, grad_packed[:, 512:], preferred_element_type=f32).astype(bf16).reshape(16, 32, 512),
        ],
        axis=1,
    ).reshape(32, 32, 512)
    arrived = lax.all_to_all(returning, DP, split_axis=0, concat_axis=0, tiled=True)
    summed, arrived = lax.optimization_barrier((summed, arrived))
    token_grads = jnp.dot(
        route, arrived.reshape(1024, 512), preferred_element_type=f32
    ).astype(bf16)

    normed_mine, normal, inverse = norm(
        z[None], patches, summed, merge_gain, merge_shift
    )
    weight, normed_mine = gather_chips(lines, normed_mine)
    merged = lax.all_gather(normed_mine, ("c", "z"), axis=0, tiled=True)

    def back(grads):
        return lax.dot_general(
            grads, weight, (((1,), (1,)), ((), ())), preferred_element_type=f32
        ).astype(bf16)

    by_core = token_grads.reshape(2, 256, 512)
    given = lax.ppermute(back(pick_core(by_core, 1 - core)), "c", SWAP)
    chip_grads = (back(pick_core(by_core, core)).astype(f32) + given.astype(f32)).astype(bf16)

    projected = jnp.dot(merged, weight, preferred_element_type=f32).astype(bf16)
    outgoing = lax.dot_general(
        route, projected, (((0,), (0,)), ((), ())), preferred_element_type=f32
    ).astype(bf16)

    first_x, first_y, chip_grads = weight_blocks(merged, token_grads, chip_grads)
    running, outgoing = scatter_chips((first_x, first_y), outgoing)
    incoming = lax.all_to_all(
        outgoing.reshape(32, 32, 512), DP, split_axis=0, concat_axis=0, tiled=True
    ).reshape(16, 2, 512 // 16, 512)
    visual = jnp.concatenate(
        [
            lax.dot_general(
                pack,
                incoming[:, h].reshape(512, 512),
                (((0,), (0,)), ((), ())),
                preferred_element_type=f32,
            ).astype(bf16)
            for h in range(2)
        ],
        axis=1,
    )

    merged_grads = lax.psum_scatter(chip_grads, "z", scatter_dimension=0, tiled=True)
    grad_layer = layer_grad(merged_grads, normal, inverse, merge_gain)

    sums, grad_layer = exchange_chips(running, grad_layer)
    chip_rows = jnp.concatenate(sums, axis=1).reshape(2, 160, 512) * (1.0 / math.sqrt(8192))
    mine = lax.dynamic_index_in_dim(chip_rows, core, 0, keepdims=False)
    other = lax.ppermute(
        lax.dynamic_index_in_dim(chip_rows, 1 - core, 0, keepdims=False), "c", SWAP
    )
    grad_weight = jnp.where(
        core == 0,
        jnp.concatenate([mine, other], axis=1),
        jnp.concatenate([other, mine], axis=1),
    )
    return (visual, grad_weight, grad_layer)


def solution(mesh):
    grid = Mesh(mesh.devices.reshape(4, 4, 2, 8), ("x", "y", "c", "z"))
    in_specs = (
        P(DP, None),
        P(),
        P(None, "z"),
        P("z", None),
        P(),
        P(),
        P(DP, "z"),
        P(),
        P(DP, "z"),
    )
    out_specs = (P(DP, "z"), P(DP, "z"), P((*DP, "z"), None))
    return jax.shard_map(body, mesh=grid, in_specs=in_specs, out_specs=out_specs, check_vma=False)
```

```python
import math

import jax
import jax.numpy as jnp
from jax import lax
from jax.sharding import Mesh
from jax.sharding import PartitionSpec as P

epsilon = 1e-06
bf16 = jnp.bfloat16
f32 = jnp.float32
DP = ("x", "y", "c")
SWAP = [(0, 1), (1, 0)]


def layer_norm(values, gain, shift):
    average = jnp.mean(values, axis=-1, keepdims=True)
    centered = values - average
    variance = jnp.mean(centered * centered, axis=-1, keepdims=True)
    return centered * lax.rsqrt(variance + epsilon) * gain + shift


def quick_gelu(values):
    return values * jax.nn.sigmoid(1.702 * values)


def exclusive_sum(values):
    return jnp.cumsum(values) - values


def position(x, y, c):
    return ((x % 4) * 4 + (y % 4)) * 2 + c


def ring_pairs(axis):
    pairs = []
    for x in range(4):
        for y in range(4):
            for c in range(2):
                step = 1 - 2 * c
                to = position(x + step, y, c) if axis == "x" else position(x, y + step, c)
                pairs.append((position(x, y, c), to))
    return pairs


def pick(array, index, axis):
    return lax.dynamic_index_in_dim(array, index % 4, axis, keepdims=False)


def pick_core(array, core):
    return lax.dynamic_index_in_dim(array, core, 0, keepdims=False)


def gather_lines(block):
    place = {"x": lax.axis_index("x"), "y": lax.axis_index("y")}
    sign = 1 - 2 * lax.axis_index("c")
    lines = []
    for i, first in enumerate("yx"):
        mine = block[:, 256 * i : 256 * (i + 1)]
        line = jnp.broadcast_to(mine, (4, 320, 256))
        for k in (1, 3, 2):
            came = lax.ppermute(mine, first, [((j + k) % 4, j) for j in range(4)])
            line = lax.dynamic_update_index_in_dim(line, came, (place[first] + k) % 4, 0)
        lines.append(line)
    return lines


def gather_chips(held, after):
    place = {"x": lax.axis_index("x"), "y": lax.axis_index("y")}
    sign = 1 - 2 * lax.axis_index("c")
    pairs = {"x": ring_pairs("x"), "y": ring_pairs("y")}
    whole = jnp.zeros((4, 4, 320, 512), bf16)
    for step in range(4):
        if step == 2:
            held, after = lax.optimization_barrier((held, after))
        for i, ring in enumerate("xy"):
            if step:
                held[i] = lax.ppermute(held[i], DP, pairs[ring])
            at = (place[ring] - sign * step) % 4
            if ring == "x":
                whole = lax.dynamic_update_slice(whole, held[i][None], (at, 0, 0, 256 * i))
            else:
                whole = lax.dynamic_update_slice(whole, held[i][:, None], (0, at, 0, 256 * i))
    return whole.reshape(5120, 512), after


def scatter_chips(terms, later):
    place = [lax.axis_index("x"), lax.axis_index("y")]
    sign = 1 - 2 * lax.axis_index("c")
    pairs = [ring_pairs("x"), ring_pairs("y")]
    running = [pick(a, place[i] - sign, i) for i, a in enumerate(terms)]
    for step in range(3):
        if step == 2:
            running, later = lax.optimization_barrier((running, later))
        for i, a in enumerate(terms):
            came = lax.ppermute(running[i], DP, pairs[i])
            mine = pick(a, place[i] - sign * (2 + step), i)
            running[i] = (came.astype(f32) + mine.astype(f32)).astype(bf16)
    return running, later


def exchange_chips(running, earlier):
    place = {"x": lax.axis_index("x"), "y": lax.axis_index("y")}
    sums = []
    for line, other in zip(running, "yx"):
        terms = [pick(line, place[other], 0)]
        for k in (1, 3, 2):
            block = pick(line, place[other] + k, 0)
            terms.append(lax.ppermute(block, other, [(j, (j + k) % 4) for j in range(4)]))
        if other == "x":
            terms, earlier = lax.optimization_barrier((terms, earlier))
        sums.append(sum(t.astype(f32) for t in terms))
    return sums, earlier


def body(patches, vit_gain, fc_in, fc_out, merge_gain, merge_shift, merger, counts, grad_packed):
    core = lax.axis_index("c")
    chip = lax.axis_index("x") * 4 + lax.axis_index("y")
    me = chip * 2 + core
    z = lax.axis_index("z")

    halves = merger.reshape(160, 2, 512)
    kept = lax.dynamic_index_in_dim(halves, core, 1, keepdims=False)
    given = lax.dynamic_index_in_dim(halves, 1 - core, 1, keepdims=False)
    got = lax.ppermute(given, "c", SWAP)
    both = jnp.where(core == 0, jnp.concatenate([kept, got]), jnp.concatenate([got, kept]))
    lines = gather_lines(both)

    inputs = patches.astype(f32)
    normed = layer_norm(inputs, vit_gain, 0.0).astype(bf16)
    hidden = quick_gelu(jnp.dot(normed, fc_in, preferred_element_type=f32)).astype(bf16)
    summed = lax.psum_scatter(
        jnp.dot(hidden, fc_out, preferred_element_type=f32).astype(bf16),
        "z",
        scatter_dimension=0,
        tiled=True,
    )

    slot = jnp.arange(16, dtype=jnp.int32)
    recv_counts = lax.dynamic_index_in_dim(counts, me, 1, keepdims=False)
    recv_start = exclusive_sum(recv_counts)
    packed_row = jnp.where(
        slot[None, :] < recv_counts[:, None], recv_start[:, None] + slot[None, :], -1
    ).reshape(512)
    pack = (packed_row[:, None] == jnp.arange(512, dtype=jnp.int32)[None, :]).astype(bf16)
    send_counts = lax.dynamic_slice_in_dim(counts, chip * 2, 2, 0)
    send_start = jnp.cumsum(send_counts, axis=1) - send_counts
    base = 256 * jnp.arange(2, dtype=jnp.int32)
    first = send_start.T[:, :, None] + slot + base[None, :, None]
    token = jnp.where(slot < send_counts.T[:, :, None], first, -1).reshape(1024)
    route = (jnp.arange(512, dtype=jnp.int32)[:, None] == token[None, :]).astype(bf16)

    returning = jnp.stack(
        [
            jnp.dot(pack, grad_packed[:, :512], preferred_element_type=f32).astype(bf16).reshape(16, 32, 512),
            jnp.dot(pack, grad_packed[:, 512:], preferred_element_type=f32).astype(bf16).reshape(16, 32, 512),
        ],
        axis=1,
    ).reshape(32, 32, 512)
    arrived = lax.all_to_all(returning, DP, split_axis=0, concat_axis=0, tiled=True)
    summed, arrived = lax.optimization_barrier((summed, arrived))
    token_grads = jnp.dot(
        route, arrived.reshape(1024, 512), preferred_element_type=f32
    ).astype(bf16)

    mine = lax.dynamic_slice_in_dim(patches, z * 128, 128, 0)
    layer_out = mine.astype(f32) + summed.astype(f32)
    average = jnp.mean(layer_out, axis=-1, keepdims=True)
    centered = layer_out - average
    inverse = lax.rsqrt(jnp.mean(centered * centered, axis=-1, keepdims=True) + epsilon)
    normal = centered * inverse
    normed_mine = (normal * merge_gain + merge_shift).astype(bf16)
    weight, normed_mine = gather_chips(lines, normed_mine)
    merged = lax.all_gather(normed_mine.reshape(32, 5120), ("c", "z"), axis=0, tiled=True)

    def back(grads):
        return lax.dot_general(
            grads, weight, (((1,), (1,)), ((), ())), preferred_element_type=f32
        ).astype(bf16)

    by_core = token_grads.reshape(2, 256, 512)
    given = lax.ppermute(back(pick_core(by_core, 1 - core)), "c", SWAP)
    chip_grads = (back(pick_core(by_core, core)).astype(f32) + given.astype(f32)).astype(bf16)

    projected = jnp.dot(merged, weight, preferred_element_type=f32).astype(bf16)
    outgoing = lax.dot_general(
        route, projected, (((0,), (0,)), ((), ())), preferred_element_type=f32
    ).astype(bf16)

    terms = [
        lax.dot_general(merged, g, (((0,), (0,)), ((), ())), preferred_element_type=f32)
        .astype(bf16)
        .reshape(4, 4, 320, 256)
        for g in (token_grads[:, :256], token_grads[:, 256:])
    ]
    terms[0], chip_grads = lax.optimization_barrier((terms[0], chip_grads))
    running, outgoing = scatter_chips(terms, outgoing)
    incoming = lax.all_to_all(
        outgoing.reshape(32, 32, 512), DP, split_axis=0, concat_axis=0, tiled=True
    ).reshape(16, 2, 512 // 16, 512)
    visual = jnp.concatenate(
        [
            lax.dot_general(
                pack,
                incoming[:, h].reshape(512, 512),
                (((0,), (0,)), ((), ())),
                preferred_element_type=f32,
            ).astype(bf16)
            for h in range(2)
        ],
        axis=1,
    )

    merged_grads = (
        lax.psum_scatter(chip_grads, "z", scatter_dimension=0, tiled=True)
        .astype(f32)
        .reshape(128, 1280)
    )
    scaled = merged_grads * merge_gain
    grad_layer = inverse * (
        scaled
        - jnp.mean(scaled, axis=-1, keepdims=True)
        - normal * jnp.mean(scaled * normal, axis=-1, keepdims=True)
    )

    sums, grad_layer = exchange_chips(running, grad_layer)
    chip_rows = jnp.concatenate(sums, axis=1).reshape(2, 160, 512) * (1.0 / math.sqrt(8192))
    mine = lax.dynamic_index_in_dim(chip_rows, core, 0, keepdims=False)
    other = lax.ppermute(
        lax.dynamic_index_in_dim(chip_rows, 1 - core, 0, keepdims=False), "c", SWAP
    )
    grad_weight = jnp.where(
        core == 0,
        jnp.concatenate([mine, other], axis=1),
        jnp.concatenate([other, mine], axis=1),
    )
    return (visual, grad_weight, grad_layer)


def solution(mesh):
    grid = Mesh(mesh.devices.reshape(4, 4, 2, 8), ("x", "y", "c", "z"))
    in_specs = (
        P(DP, None),
        P(),
        P(None, "z"),
        P("z", None),
        P(),
        P(),
        P(DP, "z"),
        P(),
        P(DP, "z"),
    )
    out_specs = (P(DP, "z"), P(DP, "z"), P((*DP, "z"), None))
    return jax.shard_map(body, mesh=grid, in_specs=in_specs, out_specs=out_specs, check_vma=False)
```

```python
import math

import jax
import jax.numpy as jnp
from jax import lax
from jax.experimental import pallas as pl
from jax.experimental.pallas import tpu as pltpu
from jax.sharding import Mesh
from jax.sharding import PartitionSpec as P

epsilon = 1e-06
bf16 = jnp.bfloat16
f32 = jnp.float32
DP = ("x", "y", "c")
SWAP = [(0, 1), (1, 0)]
VMEM = 60 * 2**20


def vision_kernel(patches, gain, fc_in, fc_out, out):
    for r in range(0, patches.shape[0], 256):
        values = patches[r : r + 256, :].astype(f32)
        centered = values - jnp.mean(values, axis=-1, keepdims=True)
        variance = jnp.mean(centered * centered, axis=-1, keepdims=True)
        normed = (centered * lax.rsqrt(variance + epsilon) * gain[...]).astype(bf16)
        hidden = jnp.dot(normed, fc_in[...], preferred_element_type=f32)
        hidden = (hidden * jax.nn.sigmoid(1.702 * hidden)).astype(bf16)
        term = jnp.dot(hidden, fc_out[...], preferred_element_type=f32)
        out[r : r + 256, :] = term.astype(bf16)


def vision(patches, gain, fc_in, fc_out):
    rows, width = patches.shape
    tile = pl.BlockSpec((512, width), lambda i: (i, 0))
    return pl.pallas_call(
        vision_kernel,
        out_shape=jax.ShapeDtypeStruct((rows, width), bf16),
        grid=(rows // 512,),
        in_specs=[tile, pl.BlockSpec((width,), lambda i: (0,))]
        + [pl.BlockSpec(a.shape, lambda i: (0, 0)) for a in (fc_in, fc_out)],
        out_specs=tile,
        compiler_params=pltpu.CompilerParams(vmem_limit_bytes=VMEM),
        cost_estimate=pl.CostEstimate(flops=4 * rows * width * 640, bytes_accessed=9 * 2**20, transcendentals=rows * 640),
        name="vision",
    )(patches, gain, fc_in, fc_out)


def norm_kernel(z, patches, summed, gain, shift, tokens, normal, inverse, held):
    layer_out = patches[...].astype(f32) + summed[...].astype(f32)
    centered = layer_out - jnp.mean(layer_out, axis=-1, keepdims=True)
    scale = lax.rsqrt(jnp.mean(centered * centered, axis=-1, keepdims=True) + epsilon)
    normal[...] = centered * scale
    inverse[...] = jnp.broadcast_to(scale, inverse.shape)
    held[...] = (normal[...] * gain[...] + shift[...]).reshape(held.shape)
    for j in range(4):
        tokens[:, 1280 * j : 1280 * (j + 1)] = held[:, j, :].astype(bf16)


def norm(z, patches, summed, gain, shift):
    fixed = lambda i, z: (0, 0)
    row = pl.BlockSpec((1280,), lambda i, z: (0,))
    return pl.pallas_call(
        norm_kernel,
        out_shape=[
            jax.ShapeDtypeStruct((32, 5120), bf16),
            jax.ShapeDtypeStruct((128, 1280), f32),
            jax.ShapeDtypeStruct((128, 128), f32),
        ],
        grid_spec=pltpu.PrefetchScalarGridSpec(
            num_scalar_prefetch=1,
            grid=(1,),
            in_specs=[
                pl.BlockSpec((128, 1280), lambda i, z: (z[0], 0)),
                pl.BlockSpec((128, 1280), fixed),
                row,
                row,
            ],
            out_specs=[
                pl.BlockSpec((32, 5120), fixed),
                pl.BlockSpec((128, 1280), fixed),
                pl.BlockSpec((128, 128), fixed),
            ],
            scratch_shapes=[pltpu.VMEM((32, 4, 1280), f32)],
        ),
        compiler_params=pltpu.CompilerParams(vmem_limit_bytes=VMEM),
        name="norm",
    )(z, patches, summed, gain, shift)


def grad_kernel(grads, normal, inverse, gain, out, held):
    for j in range(4):
        held[:, j, :] = grads[:, 1280 * j : 1280 * (j + 1)].astype(f32)
    scaled = held[...].reshape(128, 1280) * gain[...]
    unit = normal[...]
    inner = jnp.mean(scaled * unit, axis=-1, keepdims=True)
    out[...] = inverse[:, :1] * (scaled - jnp.mean(scaled, axis=-1, keepdims=True) - unit * inner)


def layer_grad(grads, normal, inverse, gain):
    return pl.pallas_call(
        grad_kernel,
        out_shape=jax.ShapeDtypeStruct((128, 1280), f32),
        scratch_shapes=[pltpu.VMEM((32, 4, 1280), f32)],
        compiler_params=pltpu.CompilerParams(vmem_limit_bytes=VMEM),
        name="layer_grad",
    )(grads, normal, inverse, gain)


def exclusive_sum(values):
    return jnp.cumsum(values) - values


def position(x, y, c):
    return (x * 4 + y) * 2 + c


def mask(c, turn):
    return 1 + 2 * ((c + turn) % 2)


def swap(array, axis, turn):
    pairs = []
    for x in range(4):
        for y in range(4):
            for c in range(2):
                m = mask(c, turn)
                to = position(x ^ m, y, c) if axis == "x" else position(x, y ^ m, c)
                pairs.append((position(x, y, c), to))
    return lax.ppermute(array, DP, pairs)


def places():
    c = lax.axis_index("c")
    return {"x": lax.axis_index("x"), "y": lax.axis_index("y")}, mask(c, 0), mask(c, 1)


def pick(array, index):
    return lax.dynamic_index_in_dim(array, index, 0, keepdims=False)


def gather_lines(block):
    place, near, far = places()
    lines = []
    for i, axis in enumerate("yx"):
        at = place[axis]
        mine = block[:, 256 * i : 256 * (i + 1)]
        one = swap(mine, axis, 0)
        two = swap(jnp.stack([mine, one]), axis, 1)
        line = jnp.broadcast_to(mine, (4, 320, 256))
        for index, part in ((at ^ near, one), (at ^ far, two[0]), (at ^ 2, two[1])):
            line = lax.dynamic_update_index_in_dim(line, part, index, 0)
        lines.append(line)
    return lines


def gather_chips(lines, after):
    place, near, far = places()
    ones = [swap(line, axis, 0) for line, axis in zip(lines, "xy")]
    lines, ones, after = lax.optimization_barrier((lines, ones, after))
    whole = jnp.zeros((4, 4, 320, 512), bf16)
    for i, axis in enumerate("xy"):
        at = place[axis]
        two = swap(jnp.stack([lines[i], ones[i]]), axis, 1)
        for index, part in ((at, lines[i]), (at ^ near, ones[i]), (at ^ far, two[0]), (at ^ 2, two[1])):
            if axis == "x":
                whole = lax.dynamic_update_slice(whole, part[None], (index, 0, 0, 256 * i))
            else:
                whole = lax.dynamic_update_slice(whole, part[:, None], (0, index, 0, 256 * i))
    return whole.reshape(5120, 512), after


def weight_kernel(order, tokens, grads, give_x, keep_x, give_y, keep_y, held):
    total = lax.dot_general(
        tokens[...], grads[...], (((0,), (0,)), ((), ())), preferred_element_type=f32
    ).astype(bf16)

    @pl.when(pl.program_id(0) < 2)
    def _():
        give_x[0] = total[:, :256]

    @pl.when(pl.program_id(0) >= 2)
    def _():
        keep_x[0] = total[:, :256]

    held[...] = total[:, 256:]

    def rows(m):
        return held[pl.ds(pl.multiple_of(order[4 + m] * 320, 64), 320), :]

    for m in range(2):
        give_y[m, 0] = rows(m)
        keep_y[m, 0] = rows(2 + m)


def weight_blocks(tokens, grads, later):
    place, near, far = places()
    masks = jnp.stack([far, 2, 0, near])
    order = jnp.concatenate([place["x"] ^ masks, place["y"] ^ masks]).astype(jnp.int32)
    flat = jax.ShapeDtypeStruct((2, 1280, 256), bf16)
    deep = jax.ShapeDtypeStruct((2, 4, 320, 256), bf16)
    give_x, keep_x, give_y, keep_y = pl.pallas_call(
        weight_kernel,
        out_shape=[flat, flat, deep, deep],
        grid_spec=pltpu.PrefetchScalarGridSpec(
            num_scalar_prefetch=1,
            grid=(4,),
            in_specs=[
                pl.BlockSpec((512, 1280), lambda k, o: (0, o[k])),
                pl.BlockSpec((512, 512), lambda k, o: (0, 0)),
            ],
            out_specs=[
                pl.BlockSpec((1, 1280, 256), lambda k, o: (jnp.minimum(k, 1), 0, 0)),
                pl.BlockSpec((1, 1280, 256), lambda k, o: (jnp.maximum(k - 2, 0), 0, 0)),
            ]
            + [pl.BlockSpec((2, 1, 320, 256), lambda k, o: (0, o[k], 0, 0))] * 2,
            scratch_shapes=[pltpu.VMEM((1280, 256), bf16)],
        ),
        compiler_params=pltpu.CompilerParams(vmem_limit_bytes=VMEM),
        cost_estimate=pl.CostEstimate(flops=16 * 512 * 1280 * 256, bytes_accessed=11 * 2**20, transcendentals=0),
        name="weight_product",
    )(order, tokens, grads)
    give_x, later = lax.optimization_barrier((give_x, later))
    along_x = [p.reshape(2, 4, 320, 256) for p in (give_x, keep_x)]
    return along_x, (give_y, keep_y), later


def scatter_chips(blocks, later):
    came = [swap(give, axis, 1) for (give, _), axis in zip(blocks, "xy")]
    passed = [
        (c[1].astype(f32) + keep[1].astype(f32)).astype(bf16) for c, (_, keep) in zip(came, blocks)
    ]
    passed, later = lax.optimization_barrier((passed, later))
    last = [swap(p, axis, 0) for p, axis in zip(passed, "xy")]
    sums = [
        (c[0].astype(f32) + keep[0].astype(f32) + end.astype(f32)).astype(bf16)
        for c, (_, keep), end in zip(came, blocks, last)
    ]
    return sums, later


def exchange_chips(running, earlier):
    place, near, far = places()
    sums = []
    for line, axis in zip(running, "yx"):
        at = place[axis]
        came = swap(jnp.stack([pick(line, at ^ far), pick(line, at ^ 2)]), axis, 1)
        passed = (came[1].astype(f32) + pick(line, at ^ near).astype(f32)).astype(bf16)
        end = swap(passed, axis, 0)
        if axis == "x":
            end, earlier = lax.optimization_barrier((end, earlier))
        sums.append(came[0].astype(f32) + pick(line, at).astype(f32) + end.astype(f32))
    return sums, earlier


def body(patches, vit_gain, fc_in, fc_out, merge_gain, merge_shift, merger, counts, grad_packed):
    core = lax.axis_index("c")
    chip = lax.axis_index("x") * 4 + lax.axis_index("y")
    me = chip * 2 + core
    z = lax.axis_index("z")

    halves = merger.reshape(160, 2, 512)
    kept = lax.dynamic_index_in_dim(halves, core, 1, keepdims=False)
    given = lax.dynamic_index_in_dim(halves, 1 - core, 1, keepdims=False)
    got = lax.ppermute(given, "c", SWAP)
    both = jnp.where(core == 0, jnp.concatenate([kept, got]), jnp.concatenate([got, kept]))
    lines = gather_lines(both)

    summed = lax.psum_scatter(
        vision(patches, vit_gain, fc_in, fc_out), "z", scatter_dimension=0, tiled=True
    )

    slot = jnp.arange(16, dtype=jnp.int32)
    recv_counts = lax.dynamic_index_in_dim(counts, me, 1, keepdims=False)
    recv_start = exclusive_sum(recv_counts)
    packed_row = jnp.where(
        slot[None, :] < recv_counts[:, None], recv_start[:, None] + slot[None, :], -1
    ).reshape(512)
    pack = (packed_row[:, None] == jnp.arange(512, dtype=jnp.int32)[None, :]).astype(bf16)
    send_counts = lax.dynamic_slice_in_dim(counts, chip * 2, 2, 0)
    send_start = jnp.cumsum(send_counts, axis=1) - send_counts
    base = 256 * jnp.arange(2, dtype=jnp.int32)
    first = send_start.T[:, :, None] + slot + base[None, :, None]
    token = jnp.where(slot < send_counts.T[:, :, None], first, -1).reshape(1024)
    route = (jnp.arange(512, dtype=jnp.int32)[:, None] == token[None, :]).astype(bf16)

    returning = jnp.stack(
        [
            jnp.dot(pack, grad_packed[:, :512], preferred_element_type=f32).astype(bf16).reshape(16, 32, 512),
            jnp.dot(pack, grad_packed[:, 512:], preferred_element_type=f32).astype(bf16).reshape(16, 32, 512),
        ],
        axis=1,
    ).reshape(32, 32, 512)
    arrived = lax.all_to_all(returning, DP, split_axis=0, concat_axis=0, tiled=True)
    summed, arrived = lax.optimization_barrier((summed, arrived))
    token_grads = jnp.dot(
        route, arrived.reshape(1024, 512), preferred_element_type=f32
    ).astype(bf16)

    normed_mine, normal, inverse = norm(
        z[None], patches, summed, merge_gain, merge_shift
    )
    weight, normed_mine = gather_chips(lines, normed_mine)
    merged = lax.all_gather(normed_mine, ("c", "z"), axis=0, tiled=True)

    def back(grads):
        return lax.dot_general(
            grads, weight, (((1,), (1,)), ((), ())), preferred_element_type=f32
        ).astype(bf16)

    by_core = token_grads.reshape(2, 256, 512)
    given = lax.ppermute(back(pick(by_core, 1 - core)), "c", SWAP)
    chip_grads = (back(pick(by_core, core)).astype(f32) + given.astype(f32)).astype(bf16)

    projected = jnp.dot(merged, weight, preferred_element_type=f32).astype(bf16)
    outgoing = lax.dot_general(
        route, projected, (((0,), (0,)), ((), ())), preferred_element_type=f32
    ).astype(bf16)

    first_x, first_y, chip_grads = weight_blocks(merged, token_grads, chip_grads)
    running, outgoing = scatter_chips((first_x, first_y), outgoing)
    incoming = lax.all_to_all(
        outgoing.reshape(32, 32, 512), DP, split_axis=0, concat_axis=0, tiled=True
    ).reshape(16, 2, 512 // 16, 512)
    visual = jnp.concatenate(
        [
            lax.dot_general(
                pack,
                incoming[:, h].reshape(512, 512),
                (((0,), (0,)), ((), ())),
                preferred_element_type=f32,
            ).astype(bf16)
            for h in range(2)
        ],
        axis=1,
    )

    merged_grads = lax.psum_scatter(chip_grads, "z", scatter_dimension=0, tiled=True)
    grad_layer = layer_grad(merged_grads, normal, inverse, merge_gain)

    sums, grad_layer = exchange_chips(running, grad_layer)
    chip_rows = jnp.concatenate(sums, axis=1).reshape(2, 160, 512) * (1.0 / math.sqrt(8192))
    mine = pick(chip_rows, core)
    other = lax.ppermute(
        pick(chip_rows, 1 - core), "c", SWAP
    )
    grad_weight = jnp.where(
        core == 0,
        jnp.concatenate([mine, other], axis=1),
        jnp.concatenate([other, mine], axis=1),
    )
    return (visual, grad_weight, grad_layer)


def solution(mesh):
    grid = Mesh(mesh.devices.reshape(4, 4, 2, 8), ("x", "y", "c", "z"))
    in_specs = (
        P(DP, None),
        P(),
        P(None, "z"),
        P("z", None),
        P(),
        P(),
        P(DP, "z"),
        P(),
        P(DP, "z"),
    )
    out_specs = (P(DP, "z"), P(DP, "z"), P((*DP, "z"), None))
    return jax.shard_map(body, mesh=grid, in_specs=in_specs, out_specs=out_specs, check_vma=False)
```

```python
import math

import jax
import jax.numpy as jnp
from jax import lax
from jax.experimental import pallas as pl
from jax.experimental.pallas import tpu as pltpu
from jax.sharding import Mesh
from jax.sharding import PartitionSpec as P

epsilon = 1e-06
bf16 = jnp.bfloat16
f32 = jnp.float32
DP = ("x", "y", "c")
SWAP = [(0, 1), (1, 0)]
VMEM = 60 * 2**20


def vision_kernel(patches, gain, fc_in, fc_out, out):
    for r in range(0, patches.shape[0], 256):
        values = patches[r : r + 256, :].astype(f32)
        centered = values - jnp.mean(values, axis=-1, keepdims=True)
        variance = jnp.mean(centered * centered, axis=-1, keepdims=True)
        normed = (centered * lax.rsqrt(variance + epsilon) * gain[...]).astype(bf16)
        hidden = jnp.dot(normed, fc_in[...], preferred_element_type=f32)
        hidden = (hidden * jax.nn.sigmoid(1.702 * hidden)).astype(bf16)
        term = jnp.dot(hidden, fc_out[...], preferred_element_type=f32)
        out[r : r + 256, :] = term.astype(bf16)


def vision(patches, gain, fc_in, fc_out):
    rows, width = patches.shape
    tile = pl.BlockSpec((512, width), lambda i: (i, 0))
    return pl.pallas_call(
        vision_kernel,
        out_shape=jax.ShapeDtypeStruct((rows, width), bf16),
        grid=(rows // 512,),
        in_specs=[tile, pl.BlockSpec((width,), lambda i: (0,))]
        + [pl.BlockSpec(a.shape, lambda i: (0, 0)) for a in (fc_in, fc_out)],
        out_specs=tile,
        compiler_params=pltpu.CompilerParams(vmem_limit_bytes=VMEM),
        cost_estimate=pl.CostEstimate(flops=4 * rows * width * 640, bytes_accessed=9 * 2**20, transcendentals=rows * 640),
        name="vision",
    )(patches, gain, fc_in, fc_out)


def norm_kernel(z, patches, summed, gain, shift, tokens, normal, inverse, held):
    layer_out = patches[...].astype(f32) + summed[...].astype(f32)
    centered = layer_out - jnp.mean(layer_out, axis=-1, keepdims=True)
    scale = lax.rsqrt(jnp.mean(centered * centered, axis=-1, keepdims=True) + epsilon)
    unit = centered * scale
    normal[...] = unit
    inverse[...] = jnp.broadcast_to(scale, inverse.shape)
    for i in range(10):
        at = slice(128 * i, 128 * (i + 1))
        held[i] = unit[:, at] * gain[at] + shift[at]
    for j in range(4):
        for i in range(10):
            at = slice(1280 * j + 128 * i, 1280 * j + 128 * (i + 1))
            tokens[:, at] = held[i, pl.ds(j, 32, stride=4), :].astype(bf16)


def norm(z, patches, summed, gain, shift):
    fixed = lambda i, z: (0, 0)
    row = pl.BlockSpec((1280,), lambda i, z: (0,))
    return pl.pallas_call(
        norm_kernel,
        out_shape=[
            jax.ShapeDtypeStruct((32, 5120), bf16),
            jax.ShapeDtypeStruct((128, 1280), f32),
            jax.ShapeDtypeStruct((128, 128), f32),
        ],
        grid_spec=pltpu.PrefetchScalarGridSpec(
            num_scalar_prefetch=1,
            grid=(1,),
            in_specs=[
                pl.BlockSpec((128, 1280), lambda i, z: (z[0], 0)),
                pl.BlockSpec((128, 1280), fixed),
                row,
                row,
            ],
            out_specs=[
                pl.BlockSpec((32, 5120), fixed),
                pl.BlockSpec((128, 1280), fixed),
                pl.BlockSpec((128, 128), fixed),
            ],
            scratch_shapes=[pltpu.VMEM((10, 128, 128), f32)],
        ),
        compiler_params=pltpu.CompilerParams(vmem_limit_bytes=VMEM),
        name="norm",
    )(z, patches, summed, gain, shift)


def grad_kernel(grads, normal, inverse, gain, out, held):
    for j in range(4):
        for i in range(10):
            at = slice(1280 * j + 128 * i, 1280 * j + 128 * (i + 1))
            held[i, pl.ds(j, 32, stride=4), :] = grads[:, at].astype(f32)
    scaled = jnp.concatenate([held[i] for i in range(10)], axis=1) * gain[...]
    unit = normal[...]
    inner = jnp.mean(scaled * unit, axis=-1, keepdims=True)
    out[...] = inverse[:, :1] * (scaled - jnp.mean(scaled, axis=-1, keepdims=True) - unit * inner)


def layer_grad(grads, normal, inverse, gain):
    return pl.pallas_call(
        grad_kernel,
        out_shape=jax.ShapeDtypeStruct((128, 1280), f32),
        scratch_shapes=[pltpu.VMEM((10, 128, 128), f32)],
        compiler_params=pltpu.CompilerParams(vmem_limit_bytes=VMEM),
        name="layer_grad",
    )(grads, normal, inverse, gain)


def exclusive_sum(values):
    return jnp.cumsum(values) - values


def position(x, y, c):
    return (x * 4 + y) * 2 + c


def mask(c, turn):
    return 1 + 2 * ((c + turn) % 2)


def swap(array, axis, turn):
    pairs = []
    for x in range(4):
        for y in range(4):
            for c in range(2):
                m = mask(c, turn)
                to = position(x ^ m, y, c) if axis == "x" else position(x, y ^ m, c)
                pairs.append((position(x, y, c), to))
    return lax.ppermute(array, DP, pairs)


def places():
    c = lax.axis_index("c")
    return {"x": lax.axis_index("x"), "y": lax.axis_index("y")}, mask(c, 0), mask(c, 1)


def pick(array, index):
    return lax.dynamic_index_in_dim(array, index, 0, keepdims=False)


def gather_lines(block):
    place, near, far = places()
    lines = []
    for i, axis in enumerate("yx"):
        at = place[axis]
        mine = block[:, 256 * i : 256 * (i + 1)]
        one = swap(mine, axis, 0)
        two = swap(jnp.stack([mine, one]), axis, 1)
        line = jnp.broadcast_to(mine, (4, 320, 256))
        for index, part in ((at ^ near, one), (at ^ far, two[0]), (at ^ 2, two[1])):
            line = lax.dynamic_update_index_in_dim(line, part, index, 0)
        lines.append(line)
    return lines


def gather_chips(lines, after):
    place, near, far = places()
    ones = [swap(line, axis, 0) for line, axis in zip(lines, "xy")]
    lines, ones, after = lax.optimization_barrier((lines, ones, after))
    whole = jnp.zeros((4, 4, 320, 512), bf16)
    for i, axis in enumerate("xy"):
        at = place[axis]
        two = swap(jnp.stack([lines[i], ones[i]]), axis, 1)
        for index, part in ((at, lines[i]), (at ^ near, ones[i]), (at ^ far, two[0]), (at ^ 2, two[1])):
            if axis == "x":
                whole = lax.dynamic_update_slice(whole, part[None], (index, 0, 0, 256 * i))
            else:
                whole = lax.dynamic_update_slice(whole, part[:, None], (0, index, 0, 256 * i))
    return whole.reshape(5120, 512), after


def weight_kernel(order, tokens, grads, give_x, own_x, next_x, give_y, own_y, next_y, held):
    total = lax.dot_general(
        tokens[...], grads[...], (((0,), (0,)), ((), ())), preferred_element_type=f32
    ).astype(bf16)

    @pl.when(pl.program_id(0) < 2)
    def _():
        give_x[0] = total[:, :256]

    @pl.when(pl.program_id(0) == 2)
    def _():
        own_x[...] = total[:, :256]

    @pl.when(pl.program_id(0) == 3)
    def _():
        next_x[...] = total[:, :256]

    held[...] = total[:, 256:]

    def rows(m):
        return held[pl.ds(pl.multiple_of(order[4 + m] * 320, 64), 320), :]

    give_y[0, 0] = rows(0)
    give_y[1, 0] = rows(1)
    own_y[0] = rows(2)
    next_y[0] = rows(3)


def weight_blocks(tokens, grads, later):
    place, near, far = places()
    masks = jnp.stack([far, 2, 0, near])
    order = jnp.concatenate([place["x"] ^ masks, place["y"] ^ masks]).astype(jnp.int32)
    shapes = [(2, 1280, 256)] + [(1280, 256)] * 2 + [(2, 4, 320, 256)] + [(4, 320, 256)] * 2
    give_x, own_x, next_x, give_y, own_y, next_y = pl.pallas_call(
        weight_kernel,
        out_shape=[jax.ShapeDtypeStruct(shape, bf16) for shape in shapes],
        grid_spec=pltpu.PrefetchScalarGridSpec(
            num_scalar_prefetch=1,
            grid=(4,),
            in_specs=[
                pl.BlockSpec((512, 1280), lambda k, o: (0, o[k])),
                pl.BlockSpec((512, 512), lambda k, o: (0, 0)),
            ],
            out_specs=[
                pl.BlockSpec((1, 1280, 256), lambda k, o: (jnp.minimum(k, 1), 0, 0)),
                pl.BlockSpec((1280, 256), lambda k, o: (0, 0)),
                pl.BlockSpec((1280, 256), lambda k, o: (0, 0)),
                pl.BlockSpec((2, 1, 320, 256), lambda k, o: (0, o[k], 0, 0)),
                pl.BlockSpec((1, 320, 256), lambda k, o: (o[k], 0, 0)),
                pl.BlockSpec((1, 320, 256), lambda k, o: (o[k], 0, 0)),
            ],
            scratch_shapes=[pltpu.VMEM((1280, 256), bf16)],
        ),
        compiler_params=pltpu.CompilerParams(vmem_limit_bytes=VMEM),
        cost_estimate=pl.CostEstimate(flops=16 * 512 * 1280 * 256, bytes_accessed=11 * 2**20, transcendentals=0),
        name="weight_product",
    )(order, tokens, grads)
    give_x, later = lax.optimization_barrier((give_x, later))
    along_x = give_x.reshape(2, 4, 320, 256), *(p.reshape(4, 320, 256) for p in (own_x, next_x))
    return along_x, (give_y, own_y, next_y), later


def scatter_chips(blocks):
    came = [swap(give, axis, 1) for (give, _, _), axis in zip(blocks, "xy")]
    last = [
        swap((c[1].astype(f32) + following.astype(f32)).astype(bf16), axis, 0)
        for c, (_, _, following), axis in zip(came, blocks, "xy")
    ]
    return [
        (c[0].astype(f32) + own.astype(f32) + end.astype(f32)).astype(bf16)
        for c, (_, own, _), end in zip(came, blocks, last)
    ]


def exchange_chips(running, earlier):
    place, near, far = places()
    sums = []
    for line, axis in zip(running, "yx"):
        at = place[axis]
        came = swap(jnp.stack([pick(line, at ^ far), pick(line, at ^ 2)]), axis, 1)
        passed = (came[1].astype(f32) + pick(line, at ^ near).astype(f32)).astype(bf16)
        end = swap(passed, axis, 0)
        if axis == "x":
            end, earlier = lax.optimization_barrier((end, earlier))
        sums.append(came[0].astype(f32) + pick(line, at).astype(f32) + end.astype(f32))
    return sums, earlier


def body(patches, vit_gain, fc_in, fc_out, merge_gain, merge_shift, merger, counts, grad_packed):
    core = lax.axis_index("c")
    chip = lax.axis_index("x") * 4 + lax.axis_index("y")
    me = chip * 2 + core
    z = lax.axis_index("z")

    halves = merger.reshape(160, 2, 512)
    kept = lax.dynamic_index_in_dim(halves, core, 1, keepdims=False)
    given = lax.dynamic_index_in_dim(halves, 1 - core, 1, keepdims=False)
    got = lax.ppermute(given, "c", SWAP)
    both = jnp.where(core == 0, jnp.concatenate([kept, got]), jnp.concatenate([got, kept]))
    lines = gather_lines(both)

    summed = lax.psum_scatter(
        vision(patches, vit_gain, fc_in, fc_out), "z", scatter_dimension=0, tiled=True
    )

    slot = jnp.arange(16, dtype=jnp.int32)
    recv_counts = lax.dynamic_index_in_dim(counts, me, 1, keepdims=False)
    recv_start = exclusive_sum(recv_counts)
    packed_row = jnp.where(
        slot[None, :] < recv_counts[:, None], recv_start[:, None] + slot[None, :], -1
    ).reshape(512)
    pack = (packed_row[:, None] == jnp.arange(512, dtype=jnp.int32)[None, :]).astype(bf16)
    send_counts = lax.dynamic_slice_in_dim(counts, chip * 2, 2, 0)
    send_start = jnp.cumsum(send_counts, axis=1) - send_counts
    base = 256 * jnp.arange(2, dtype=jnp.int32)
    first = send_start.T[:, :, None] + slot + base[None, :, None]
    token = jnp.where(slot < send_counts.T[:, :, None], first, -1).reshape(1024)
    route = (jnp.arange(512, dtype=jnp.int32)[:, None] == token[None, :]).astype(bf16)

    returning = jnp.stack(
        [
            jnp.dot(pack, grad_packed[:, :512], preferred_element_type=f32).astype(bf16).reshape(16, 32, 512),
            jnp.dot(pack, grad_packed[:, 512:], preferred_element_type=f32).astype(bf16).reshape(16, 32, 512),
        ],
        axis=1,
    ).reshape(32, 32, 512)
    arrived = lax.all_to_all(returning, DP, split_axis=0, concat_axis=0, tiled=True)
    summed, arrived = lax.optimization_barrier((summed, arrived))
    token_grads = jnp.dot(
        route, arrived.reshape(1024, 512), preferred_element_type=f32
    ).astype(bf16)

    normed_mine, normal, inverse = norm(
        z[None], patches, summed, merge_gain, merge_shift
    )
    weight, normed_mine = gather_chips(lines, normed_mine)
    merged = lax.all_gather(normed_mine, ("c", "z"), axis=0, tiled=True)

    def back(grads):
        return lax.dot_general(
            grads, weight, (((1,), (1,)), ((), ())), preferred_element_type=f32
        ).astype(bf16)

    by_core = token_grads.reshape(2, 256, 512)
    given = lax.ppermute(back(pick(by_core, 1 - core)), "c", SWAP)
    chip_grads = (back(pick(by_core, core)).astype(f32) + given.astype(f32)).astype(bf16)

    projected = jnp.dot(merged, weight, preferred_element_type=f32).astype(bf16)
    outgoing = lax.dot_general(
        route, projected, (((0,), (0,)), ((), ())), preferred_element_type=f32
    ).astype(bf16)

    first_x, first_y, chip_grads = weight_blocks(merged, token_grads, chip_grads)
    running = scatter_chips((first_x, first_y))
    incoming = lax.all_to_all(
        outgoing.reshape(32, 32, 512), DP, split_axis=0, concat_axis=0, tiled=True
    ).reshape(16, 2, 512 // 16, 512)
    visual = jnp.concatenate(
        [
            lax.dot_general(
                pack,
                incoming[:, h].reshape(512, 512),
                (((0,), (0,)), ((), ())),
                preferred_element_type=f32,
            ).astype(bf16)
            for h in range(2)
        ],
        axis=1,
    )

    merged_grads = lax.psum_scatter(chip_grads, "z", scatter_dimension=0, tiled=True)
    grad_layer = layer_grad(merged_grads, normal, inverse, merge_gain)

    sums, grad_layer = exchange_chips(running, grad_layer)
    chip_rows = jnp.concatenate(sums, axis=1).reshape(2, 160, 512) * (1.0 / math.sqrt(8192))
    mine = pick(chip_rows, core)
    other = lax.ppermute(
        pick(chip_rows, 1 - core), "c", SWAP
    )
    grad_weight = jnp.where(
        core == 0,
        jnp.concatenate([mine, other], axis=1),
        jnp.concatenate([other, mine], axis=1),
    )
    return (visual, grad_weight, grad_layer)


def solution(mesh):
    grid = Mesh(mesh.devices.reshape(4, 4, 2, 8), ("x", "y", "c", "z"))
    in_specs = (
        P(DP, None),
        P(),
        P(None, "z"),
        P("z", None),
        P(),
        P(),
        P(DP, "z"),
        P(),
        P(DP, "z"),
    )
    out_specs = (P(DP, "z"), P(DP, "z"), P((*DP, "z"), None))
    return jax.shard_map(body, mesh=grid, in_specs=in_specs, out_specs=out_specs, check_vma=False)
```

```python
import math

import jax
import jax.numpy as jnp
from jax import lax
from jax.experimental import pallas as pl
from jax.experimental.pallas import tpu as pltpu
from jax.sharding import Mesh
from jax.sharding import PartitionSpec as P

epsilon = 1e-06
bf16 = jnp.bfloat16
f32 = jnp.float32
DP = ("x", "y", "c")
SWAP = [(0, 1), (1, 0)]
VMEM = 60 * 2**20


def vision_kernel(patches, gain, fc_in, fc_out, out):
    for r in range(0, patches.shape[0], 256):
        values = patches[r : r + 256, :].astype(f32)
        centered = values - jnp.mean(values, axis=-1, keepdims=True)
        variance = jnp.mean(centered * centered, axis=-1, keepdims=True)
        normed = (centered * lax.rsqrt(variance + epsilon) * gain[...]).astype(bf16)
        hidden = jnp.dot(normed, fc_in[...], preferred_element_type=f32)
        hidden = (hidden * jax.nn.sigmoid(1.702 * hidden)).astype(bf16)
        term = jnp.dot(hidden, fc_out[...], preferred_element_type=f32)
        out[r : r + 256, :] = term.astype(bf16)


def vision(patches, gain, fc_in, fc_out):
    rows, width = patches.shape
    tile = pl.BlockSpec((512, width), lambda i: (i, 0))
    return pl.pallas_call(
        vision_kernel,
        out_shape=jax.ShapeDtypeStruct((rows, width), bf16),
        grid=(rows // 512,),
        in_specs=[tile, pl.BlockSpec((width,), lambda i: (0,))]
        + [pl.BlockSpec(a.shape, lambda i: (0, 0)) for a in (fc_in, fc_out)],
        out_specs=tile,
        compiler_params=pltpu.CompilerParams(vmem_limit_bytes=VMEM),
        cost_estimate=pl.CostEstimate(flops=4 * rows * width * 640, bytes_accessed=9 * 2**20, transcendentals=rows * 640),
        name="vision",
    )(patches, gain, fc_in, fc_out)


def norm_kernel(z, patches, summed, gain, shift, tokens, normal, inverse, held):
    layer_out = patches[...].astype(f32) + summed[...].astype(f32)
    centered = layer_out - jnp.mean(layer_out, axis=-1, keepdims=True)
    scale = lax.rsqrt(jnp.mean(centered * centered, axis=-1, keepdims=True) + epsilon)
    unit = centered * scale
    normal[...] = unit
    inverse[...] = jnp.broadcast_to(scale, inverse.shape)
    for i in range(10):
        at = slice(128 * i, 128 * (i + 1))
        held[i] = unit[:, at] * gain[at] + shift[at]
    for j in range(4):
        for i in range(10):
            at = slice(1280 * j + 128 * i, 1280 * j + 128 * (i + 1))
            tokens[:, at] = held[i, pl.ds(j, 32, stride=4), :].astype(bf16)


def norm(z, patches, summed, gain, shift):
    fixed = lambda i, z: (0, 0)
    row = pl.BlockSpec((1280,), lambda i, z: (0,))
    return pl.pallas_call(
        norm_kernel,
        out_shape=[
            jax.ShapeDtypeStruct((32, 5120), bf16),
            jax.ShapeDtypeStruct((128, 1280), f32),
            jax.ShapeDtypeStruct((128, 128), f32),
        ],
        grid_spec=pltpu.PrefetchScalarGridSpec(
            num_scalar_prefetch=1,
            grid=(1,),
            in_specs=[
                pl.BlockSpec((128, 1280), lambda i, z: (z[0], 0)),
                pl.BlockSpec((128, 1280), fixed),
                row,
                row,
            ],
            out_specs=[
                pl.BlockSpec((32, 5120), fixed),
                pl.BlockSpec((128, 1280), fixed),
                pl.BlockSpec((128, 128), fixed),
            ],
            scratch_shapes=[pltpu.VMEM((10, 128, 128), f32)],
        ),
        compiler_params=pltpu.CompilerParams(vmem_limit_bytes=VMEM),
        name="norm",
    )(z, patches, summed, gain, shift)


def grad_kernel(grads, normal, inverse, gain, out, held):
    for j in range(4):
        for i in range(10):
            at = slice(1280 * j + 128 * i, 1280 * j + 128 * (i + 1))
            held[i, pl.ds(j, 32, stride=4), :] = grads[:, at].astype(f32)
    scaled = jnp.concatenate([held[i] for i in range(10)], axis=1) * gain[...]
    unit = normal[...]
    inner = jnp.mean(scaled * unit, axis=-1, keepdims=True)
    out[...] = inverse[:, :1] * (scaled - jnp.mean(scaled, axis=-1, keepdims=True) - unit * inner)


def layer_grad(grads, normal, inverse, gain):
    return pl.pallas_call(
        grad_kernel,
        out_shape=jax.ShapeDtypeStruct((128, 1280), f32),
        scratch_shapes=[pltpu.VMEM((10, 128, 128), f32)],
        compiler_params=pltpu.CompilerParams(vmem_limit_bytes=VMEM),
        name="layer_grad",
    )(grads, normal, inverse, gain)


def exclusive_sum(values):
    return jnp.cumsum(values) - values


def position(x, y, c):
    return (x * 4 + y) * 2 + c


def mask(c, turn):
    return 1 + 2 * ((c + turn) % 2)


def swap(array, axis, turn):
    pairs = []
    for x in range(4):
        for y in range(4):
            for c in range(2):
                m = mask(c, turn)
                to = position(x ^ m, y, c) if axis == "x" else position(x, y ^ m, c)
                pairs.append((position(x, y, c), to))
    return lax.ppermute(array, DP, pairs)


def places():
    c = lax.axis_index("c")
    return {"x": lax.axis_index("x"), "y": lax.axis_index("y")}, mask(c, 0), mask(c, 1)


def pick(array, index):
    return lax.dynamic_index_in_dim(array, index, 0, keepdims=False)


def gather_lines(block):
    place, near, far = places()
    lines = []
    for i, axis in enumerate("yx"):
        at = place[axis]
        mine = block[:, 256 * i : 256 * (i + 1)]
        one = swap(mine, axis, 0)
        two = swap(jnp.stack([mine, one]), axis, 1)
        line = jnp.broadcast_to(mine, (4, 320, 256))
        for index, part in ((at ^ near, one), (at ^ far, two[0]), (at ^ 2, two[1])):
            line = lax.dynamic_update_index_in_dim(line, part, index, 0)
        lines.append(line)
    return lines


def gather_chips(lines, after):
    place, near, far = places()
    ones = [swap(line, axis, 0) for line, axis in zip(lines, "xy")]
    lines, ones, after = lax.optimization_barrier((lines, ones, after))
    whole = jnp.zeros((4, 4, 320, 512), bf16)
    for i, axis in enumerate("xy"):
        at = place[axis]
        two = swap(jnp.stack([lines[i], ones[i]]), axis, 1)
        for index, part in ((at, lines[i]), (at ^ near, ones[i]), (at ^ far, two[0]), (at ^ 2, two[1])):
            if axis == "x":
                whole = lax.dynamic_update_slice(whole, part[None], (index, 0, 0, 256 * i))
            else:
                whole = lax.dynamic_update_slice(whole, part[:, None], (0, index, 0, 256 * i))
    return whole.reshape(5120, 512), after


def weight_kernel(order, tokens, grads, give_x, own_x, next_x, give_y, own_y, next_y, held):
    total = lax.dot_general(
        tokens[...], grads[...], (((0,), (0,)), ((), ())), preferred_element_type=f32
    ).astype(bf16)

    @pl.when(pl.program_id(0) < 2)
    def _():
        give_x[0] = total[:, :256]

    @pl.when(pl.program_id(0) == 2)
    def _():
        own_x[...] = total[:, :256]

    @pl.when(pl.program_id(0) == 3)
    def _():
        next_x[...] = total[:, :256]

    held[...] = total[:, 256:]

    def rows(m):
        return held[pl.ds(pl.multiple_of(order[4 + m] * 320, 64), 320), :]

    give_y[0, 0] = rows(0)
    give_y[1, 0] = rows(1)
    own_y[0] = rows(2)
    next_y[0] = rows(3)


def weight_blocks(tokens, grads, later):
    place, near, far = places()
    masks = jnp.stack([far, 2, 0, near])
    order = jnp.concatenate([place["x"] ^ masks, place["y"] ^ masks]).astype(jnp.int32)
    shapes = [(2, 1280, 256)] + [(1280, 256)] * 2 + [(2, 4, 320, 256)] + [(4, 320, 256)] * 2
    give_x, own_x, next_x, give_y, own_y, next_y = pl.pallas_call(
        weight_kernel,
        out_shape=[jax.ShapeDtypeStruct(shape, bf16) for shape in shapes],
        grid_spec=pltpu.PrefetchScalarGridSpec(
            num_scalar_prefetch=1,
            grid=(4,),
            in_specs=[
                pl.BlockSpec((512, 1280), lambda k, o: (0, o[k])),
                pl.BlockSpec((512, 512), lambda k, o: (0, 0)),
            ],
            out_specs=[
                pl.BlockSpec((1, 1280, 256), lambda k, o: (jnp.minimum(k, 1), 0, 0)),
                pl.BlockSpec((1280, 256), lambda k, o: (0, 0)),
                pl.BlockSpec((1280, 256), lambda k, o: (0, 0)),
                pl.BlockSpec((2, 1, 320, 256), lambda k, o: (0, o[k], 0, 0)),
                pl.BlockSpec((1, 320, 256), lambda k, o: (o[k], 0, 0)),
                pl.BlockSpec((1, 320, 256), lambda k, o: (o[k], 0, 0)),
            ],
            scratch_shapes=[pltpu.VMEM((1280, 256), bf16)],
        ),
        compiler_params=pltpu.CompilerParams(vmem_limit_bytes=VMEM),
        cost_estimate=pl.CostEstimate(flops=16 * 512 * 1280 * 256, bytes_accessed=11 * 2**20, transcendentals=0),
        name="weight_product",
    )(order, tokens, grads)
    give_x, later = lax.optimization_barrier((give_x, later))
    along_x = give_x.reshape(2, 4, 320, 256), *(p.reshape(4, 320, 256) for p in (own_x, next_x))
    return along_x, (give_y, own_y, next_y), later


def scatter_chips(blocks):
    came = [swap(give, axis, 1) for (give, _, _), axis in zip(blocks, "xy")]
    last = [
        swap((c[1].astype(f32) + following.astype(f32)).astype(bf16), axis, 0)
        for c, (_, _, following), axis in zip(came, blocks, "xy")
    ]
    return [
        (c[0].astype(f32) + own.astype(f32) + end.astype(f32)).astype(bf16)
        for c, (_, own, _), end in zip(came, blocks, last)
    ]


def exchange_chips(running, earlier):
    place, near, far = places()
    sums = []
    for line, axis in zip(running, "yx"):
        at = place[axis]
        came = swap(jnp.stack([pick(line, at ^ far), pick(line, at ^ 2)]), axis, 1)
        passed = (came[1].astype(f32) + pick(line, at ^ near).astype(f32)).astype(bf16)
        end = swap(passed, axis, 0)
        if axis == "x":
            end, earlier = lax.optimization_barrier((end, earlier))
        sums.append(came[0].astype(f32) + pick(line, at).astype(f32) + end.astype(f32))
    return sums, earlier


def body(patches, vit_gain, fc_in, fc_out, merge_gain, merge_shift, merger, counts, grad_packed):
    core = lax.axis_index("c")
    chip = lax.axis_index("x") * 4 + lax.axis_index("y")
    me = chip * 2 + core
    z = lax.axis_index("z")

    halves = merger.reshape(160, 2, 512)
    kept = lax.dynamic_index_in_dim(halves, core, 1, keepdims=False)
    given = lax.dynamic_index_in_dim(halves, 1 - core, 1, keepdims=False)
    got = lax.ppermute(given, "c", SWAP)
    both = jnp.where(core == 0, jnp.concatenate([kept, got]), jnp.concatenate([got, kept]))
    lines = gather_lines(both)

    summed = lax.psum_scatter(
        vision(patches, vit_gain, fc_in, fc_out), "z", scatter_dimension=0, tiled=True
    )

    slot = jnp.arange(16, dtype=jnp.int32)
    recv_counts = lax.dynamic_index_in_dim(counts, me, 1, keepdims=False)
    recv_start = exclusive_sum(recv_counts)
    packed_row = jnp.where(
        slot[None, :] < recv_counts[:, None], recv_start[:, None] + slot[None, :], -1
    ).reshape(512)
    pack = (packed_row[:, None] == jnp.arange(512, dtype=jnp.int32)[None, :]).astype(bf16)
    send_counts = lax.dynamic_slice_in_dim(counts, chip * 2, 2, 0)
    send_start = jnp.cumsum(send_counts, axis=1) - send_counts
    base = 256 * jnp.arange(2, dtype=jnp.int32)
    first = send_start.T[:, :, None] + slot + base[None, :, None]
    token = jnp.where(slot < send_counts.T[:, :, None], first, -1).reshape(1024)
    route = (jnp.arange(512, dtype=jnp.int32)[:, None] == token[None, :]).astype(bf16)

    returning = jnp.stack(
        [
            jnp.dot(pack, grad_packed[:, :512], preferred_element_type=f32).astype(bf16).reshape(16, 32, 512),
            jnp.dot(pack, grad_packed[:, 512:], preferred_element_type=f32).astype(bf16).reshape(16, 32, 512),
        ],
        axis=1,
    ).reshape(32, 32, 512)
    arrived = lax.all_to_all(returning, DP, split_axis=0, concat_axis=0, tiled=True)
    summed, arrived = lax.optimization_barrier((summed, arrived))
    token_grads = jnp.dot(
        route, arrived.reshape(1024, 512), preferred_element_type=f32
    ).astype(bf16)

    normed_mine, normal, inverse = norm(
        z[None], patches, summed, merge_gain, merge_shift
    )
    weight, normed_mine = gather_chips(lines, normed_mine)
    merged = lax.all_gather(normed_mine, ("c", "z"), axis=0, tiled=True)

    def back(grads):
        return lax.dot_general(
            grads, weight, (((1,), (1,)), ((), ())), preferred_element_type=f32
        ).astype(bf16)

    by_core = token_grads.reshape(2, 256, 512)
    given = lax.ppermute(back(pick(by_core, 1 - core)), "c", SWAP)
    chip_grads = (back(pick(by_core, core)).astype(f32) + given.astype(f32)).astype(bf16)

    projected = jnp.dot(merged, weight, preferred_element_type=f32).astype(bf16)
    outgoing = lax.dot_general(
        route, projected, (((0,), (0,)), ((), ())), preferred_element_type=f32
    ).astype(bf16)

    first_x, first_y, chip_grads = weight_blocks(merged, token_grads, chip_grads)
    running = scatter_chips((first_x, first_y))
    incoming = lax.all_to_all(
        outgoing.reshape(32, 32, 512), DP, split_axis=0, concat_axis=0, tiled=True
    ).reshape(16, 2, 512 // 16, 512)
    visual = jnp.concatenate(
        [
            lax.dot_general(
                pack,
                incoming[:, h].reshape(512, 512),
                (((0,), (0,)), ((), ())),
                preferred_element_type=f32,
            ).astype(bf16)
            for h in range(2)
        ],
        axis=1,
    )

    merged_grads = lax.psum_scatter(chip_grads, "z", scatter_dimension=0, tiled=True)
    grad_layer = layer_grad(merged_grads, normal, inverse, merge_gain)

    sums, grad_layer = exchange_chips(running, grad_layer)
    mine, other = [], []
    for part in sums:
        rows = part.reshape(2, 160, 256) * (1.0 / math.sqrt(8192))
        mine.append(pick(rows, core))
        other.append(lax.ppermute(pick(rows, 1 - core), "c", SWAP))
    grad_weight = jnp.where(
        core == 0,
        jnp.concatenate(mine + other, axis=1),
        jnp.concatenate(other + mine, axis=1),
    )
    return (visual, grad_weight, grad_layer)


def solution(mesh):
    grid = Mesh(mesh.devices.reshape(4, 4, 2, 8), ("x", "y", "c", "z"))
    in_specs = (
        P(DP, None),
        P(),
        P(None, "z"),
        P("z", None),
        P(),
        P(),
        P(DP, "z"),
        P(),
        P(DP, "z"),
    )
    out_specs = (P(DP, "z"), P(DP, "z"), P((*DP, "z"), None))
    return jax.shard_map(body, mesh=grid, in_specs=in_specs, out_specs=out_specs, check_vma=False)
```
